128 devices in a mesh: lon: 16 (over x, y), lat: 8 (over z, core).
Axes of the slice: x: 4, y: 4, z: 4, core: 2. Of those that a mesh axis runs over, the one named last changes fastest.
Arguments:
- control: float32 [5, 127, 64, 2048], P(None, None, 'lat', 'lon'), may hold values from -6 to 6
- residual: float32 [5, 127, 64, 2048], P(None, None, 'lat', 'lon'), may hold values from -11 to 11
- direction: float32 [5, 127, 64, 2048], P(None, None, 'lat', 'lon'), may hold values from -11 to 11
- ensemble: bfloat16 [4, 2, 127, 64, 2048], P(None, None, None, 'lat', 'lon'), may hold values from -3 to 3
- static_std: bfloat16 [127, 64, 2048], P(None, 'lat', 'lon'), may hold values from 0.29882812 to 3
- vertical: float32 [127, 127], replicated, may hold values from 0 to 1
- owner: int32 [32768, 1], P(('lon', 'lat')), may hold values from 0 to 127; in each aligned block of 256 rows (0 to 255, 256 to 511, ...) at most 4 rows name the same one
- column: int32 [32768], P(('lon', 'lat')), may hold values from 0 to 894, as said below
- slot: int32 [32768], P(('lon', 'lat')), may hold values from 0 to 1
- corner: int32 [32768, 4], P(('lon', 'lat')), may hold values from 0 to 1, as said below
- obs_weight: float32 [32768, 127], P(('lon', 'lat')), may hold values from 0.2 to 2
- live_count: int32 [128], P(('lon', 'lat')), may hold values from 192 to 256
Outputs:
- new_control: float32 [5, 127, 64, 2048], P(None, None, 'lat', 'lon')
- new_residual: float32 [5, 127, 64, 2048], P(None, None, 'lat', 'lon')
- new_direction: float32 [5, 127, 64, 2048], P(None, None, 'lat', 'lon')
The draws below stay inside these ranges and needn't reach their ends.
Inputs may be any that keep to these rules, and one draw needn't show every extreme that they name: `owner`: within the 256 records of one device no tile is named more than 4 times. `column`: the latitude row is below 7 and the longitude cell below 127. `corner`: exactly one entry of each row is 1.
All inputs are finite; a program needn't handle non-finite values.
Results may differ from the reference program's by a relative error of at most 0.0003.
Values sent between devices are 32-bit elements; how exact they have to be, the bound alone decides.
A program may use at most 128 MiB of HBM per device.

```python
import math
import jax
import jax.numpy as jnp
import numpy as np
from jax import lax

LEV = 127
MEMBERS = 4
SLOTS = 2
CLAT = 8
CLON = 128
OBS_DEV = 256
TILES = 128
NLAT = 64
NLON = 2048
CAP = 4
NOBS = 32768
N_LAT = 8


def ramp_field():
    lat_pos = jnp.arange(NLAT, dtype=jnp.float32) / NLAT
    lon_pos = jnp.arange(NLON, dtype=jnp.float32) / NLON
    return 0.6 * jnp.power(3.0, 0.5 * lat_pos[:, None] + 0.5 * lon_pos[None, :])


def draw_residual(key, part):
    key = jax.random.fold_in(key, 11)
    shape_all = (MEMBERS + 1, LEV, NLAT, NLON)
    noise = jnp.clip(jax.random.normal(key, shape_all, jnp.float32), -6.0, 6.0) * ramp_field()
    return noise


def draw_direction(key, part):
    key = jax.random.fold_in(key, 17)
    shape_all = (MEMBERS + 1, LEV, NLAT, NLON)
    noise = jnp.clip(jax.random.normal(key, shape_all, jnp.float32), -6.0, 6.0) * ramp_field()
    return noise


def draw_vertical(key, part):
    key = jax.random.fold_in(key, 21)
    rows_pos = jnp.arange(LEV, dtype=jnp.float32)[:, None]
    cols_pos = jnp.arange(LEV, dtype=jnp.float32)[None, :]
    base = jnp.exp(-jnp.abs(rows_pos - cols_pos) / 6.0) / 2.5
    factor = jax.random.uniform(key, (LEV, LEV), jnp.float32, 0.5, 1.5)
    return base * factor


def draw_column(key, part):
    key = jax.random.fold_in(key, 31)
    key_lat, key_lon = jax.random.split(key)
    lat_row = jax.random.randint(key_lat, (NOBS,), 0, CLAT - 1)
    lon_cell = jax.random.randint(key_lon, (NOBS,), 0, CLON - 1)
    return (lat_row * CLON + lon_cell).astype(jnp.int32)


def draw_corner(key, part):
    key = jax.random.fold_in(key, 41)
    picked = jax.random.randint(key, (NOBS,), 0, 4)
    return (picked[:, None] == jnp.arange(4, dtype=jnp.int32)[None, :]).astype(jnp.int32)


def draw_live_count(key, part):
    key = jax.random.fold_in(key, 51)
    key_counts, key_full = jax.random.split(key)
    counts = jax.random.randint(key_counts, (TILES,), 3 * OBS_DEV // 4, OBS_DEV + 1)
    full_tile = jax.random.randint(key_full, (), 0, TILES)
    return counts.at[full_tile].set(OBS_DEV).astype(jnp.int32)


def place_ends(values, stream_key, least, top_value):
    place = [jax.random.randint(jax.random.fold_in(stream_key, axis), (), 0, length) for axis, length in enumerate(values.shape)]
    main_axis = values.shape.index(max(values.shape))
    neighbour = place[:main_axis] + [(place[main_axis] + 1) % values.shape[main_axis]] + place[main_axis + 1:]
    return values.at[tuple(place)].set(least).at[tuple(neighbour)].set(top_value)


def block_scale(rng, shape, shards, least, top_value):
    def one(position, shards_of):
        heights = jax.random.uniform(jax.random.fold_in(jax.random.fold_in(rng, 6), position), (shards_of,), jnp.float32, least / len(shards), top_value / len(shards))
        return jnp.repeat(jnp.exp(heights), shape[position] // shards_of).reshape((-1,) + (1,) * (len(shape) - position - 1))

    gain = one(*shards[0])
    for cut in shards[1:]:
        gain = gain * one(*cut)
    return gain


def shared_out(stream_key, own, number, rows, number_of, top, limit, skew):
    sequence = jax.random.permutation(stream_key, number_of)
    heavy_load, ordinary = load_shares(number_of, rows * top, limit, skew, True), load_shares(number_of, rows * top, limit, skew, False)
    places = jnp.arange(number_of)

    def named(lengths, turn):
        used = int((lengths > 0).sum())
        fixed = max(1, used // 4)
        passed = fixed + (places - fixed + turn * (used - fixed)) % max(1, number_of - fixed)
        return jnp.zeros((number_of,), jnp.int32).at[sequence[jnp.where(places < fixed, places, passed)]].set(jnp.asarray(lengths, jnp.int32))

    lengths = jnp.where(number % 4 == 0, named(heavy_load, number // 4), named(ordinary, number - number // 4 - 1))
    mixed = jax.random.permutation(jax.random.fold_in(own, 3), number_of)
    source_of, taker = mixed[0:number_of // 2 * 2:2], mixed[1:number_of // 2 * 2:2]
    margin = jnp.minimum(lengths[source_of] - 1, limit - lengths[taker]) // 2
    margin = jnp.where((source_of == sequence[0]) | (taker == sequence[0]) | (lengths[taker] == 0), 0, jnp.maximum(margin, 0))
    passed = jax.random.randint(jax.random.fold_in(own, 4), (number_of // 2,), 0, 1 << 20) % (margin + 1)
    lengths = lengths.at[source_of].add(-passed).at[taker].add(passed)
    members = jnp.searchsorted(jnp.cumsum(lengths), jnp.arange(rows * top), side="right").astype(jnp.int32)
    listing = members.reshape(top, rows).T
    listing = listing[jax.random.permutation(jax.random.fold_in(own, 1), rows)]
    turn = jax.random.randint(jax.random.fold_in(own, 2), (rows, 1), 0, top)
    return jnp.take_along_axis(listing, (jnp.arange(top)[None, :] + turn) % top, axis=1)


def load_shares(number_of, total, reach, slope, full):
    weights = [(1 << 20) // math.isqrt(standing ** slope) + 1 for standing in range(1, number_of + 1)]
    largest = reach if full else min(reach, max(-(-total // number_of), total * weights[0] // sum(weights)))
    least = 1 if total - largest >= number_of - 1 else 0
    given, spare = [largest] + [least] * (number_of - 1), total - largest - least * (number_of - 1)
    while spare > 0:
        movable = [i for i in range(1, number_of) if given[i] < largest] or [i for i in range(1, number_of) if given[i] < reach]
        mass, remaining = sum([weights[i] for i in movable]), spare
        for i in movable:
            more = min(reach - given[i], max(1, remaining * weights[i] // mass), spare)
            given[i] = given[i] + more
            spare = spare - more
    return np.array(given)


def normal_values(stream_key, shape, scale, reach, cuts=(), kind=jnp.bfloat16):
    entries = jax.random.normal(stream_key, shape, jnp.float32) * scale
    if len(cuts) > 0:
        entries = block_scale(stream_key, shape, cuts, -0.22, 0.18) * entries
    return jnp.clip(entries, min=-reach, max=reach).astype(kind)


def setup_inputs(seed: int = 0) -> dict:
    keys = jax.random.split(jax.random.key(seed), 13)
    control = normal_values(keys[0], (MEMBERS + 1, LEV, NLAT, NLON), 1.0, 6.0, ((2, 8), (3, 16)), jnp.float32)
    residual = draw_residual(jax.random.fold_in(keys[12], 71), 0)
    direction = draw_direction(jax.random.fold_in(keys[12], 71), 0)
    ensemble = normal_values(keys[3], (MEMBERS, SLOTS, LEV, NLAT, NLON), 0.5, 3.0, ((3, 8), (4, 16)))
    static_std = jnp.clip(jnp.exp(math.log(3.0) - 2.306499 * jax.random.uniform(keys[4], (LEV, NLAT, NLON), jnp.float32) ** block_scale(keys[4], (LEV, NLAT, NLON), ((1, 8), (2, 16)), -0.2, 0.2)), 0.29882812, 3.0).astype(jnp.bfloat16)
    vertical = draw_vertical(jax.random.fold_in(keys[12], 71), 0)
    owner_keys = jax.random.split(jax.random.fold_in(keys[6], 1), NOBS // OBS_DEV)
    owner_turns = jax.random.permutation(jax.random.fold_in(keys[6], 3), NOBS // OBS_DEV)
    owner = jax.vmap(lambda own, number: shared_out(jax.random.fold_in(keys[6], 2), own, number, OBS_DEV, TILES, 1, CAP, 2))(owner_keys, owner_turns).reshape((NOBS, 1))
    column = draw_column(jax.random.fold_in(keys[12], 71), 0)
    slot = place_ends(jax.random.randint(keys[8], (NOBS,), 0, SLOTS), jax.random.fold_in(keys[8], 1), 0, SLOTS - 1).astype(jnp.int32)
    corner = draw_corner(jax.random.fold_in(keys[12], 71), 0)
    obs_weight = jnp.clip(jnp.exp(math.log(2.0) - 2.3025851 * jax.random.uniform(keys[10], (NOBS, LEV), jnp.float32) ** block_scale(keys[10], (NOBS, LEV), ((0, 128),), -0.2, 0.2)), 0.2, 2.0)
    live_count = draw_live_count(jax.random.fold_in(keys[12], 71), 0)
    return {"control": control, "residual": residual, "direction": direction, "ensemble": ensemble, "static_std": static_std, "vertical": vertical, "owner": owner, "column": column, "slot": slot, "corner": corner, "obs_weight": obs_weight, "live_count": live_count}


def filter_taps():
    raw_taps = [math.exp(-(offset * offset) / 8.0) for offset in range(-3, 4)]
    scale_total = math.sqrt(sum((entry_value * entry_value for entry_value in raw_taps)))
    return [entry_value / scale_total for entry_value in raw_taps]

def vertical_apply(matrix, field):
    return jnp.einsum('ab,kbij->kaij', matrix, field, precision=lax.Precision.HIGHEST)

def vertical_adjoint(matrix, field):
    return jnp.einsum('ba,kbij->kaij', matrix, field, precision=lax.Precision.HIGHEST)

def smooth_field(field):
    taps = filter_taps()
    across = None
    for number, offset in enumerate(range(-3, 4)):
        term = taps[number] * jnp.roll(field, -offset, axis=3)
        across = term if across is None else across + term
    lat_total = field.shape[2]
    padded = jnp.pad(across, ((0, 0), (0, 0), (3, 3), (0, 0)))
    result = None
    for number, offset in enumerate(range(-3, 4)):
        term = taps[number] * padded[:, :, 3 + offset:3 + offset + lat_total, :]
        result = term if result is None else result + term
    return result

def reference(control, residual, direction, ensemble, static_std, vertical, owner, column, slot, corner, obs_weight, live_count):
    localized = smooth_field(vertical_apply(vertical, direction))
    increment = ensemble[0].astype(jnp.float32) * localized[0]
    for member in range(1, MEMBERS):
        increment = increment + ensemble[member].astype(jnp.float32) * localized[member]
    spread = static_std.astype(jnp.float32)
    increment = increment + 0.5 * spread * localized[MEMBERS]
    record_ids = jnp.arange(NOBS, dtype=jnp.int32)
    live = record_ids % OBS_DEV < live_count[record_ids // OBS_DEV]
    offsets = jnp.array([0, 1, CLON, CLON + 1], dtype=jnp.int32)
    inside = column + lax.optimization_barrier(jnp.sum(corner * offsets, axis=1))
    tile_ids = owner[:, 0]
    glob_lat = tile_ids % N_LAT * CLAT + inside // CLON
    glob_lon = tile_ids // N_LAT * CLON + inside % CLON
    evolved = increment[slot, :, glob_lat, glob_lon]
    weighted = jnp.where(live[:, None], obs_weight * evolved, jnp.zeros_like(evolved))
    back = jnp.zeros_like(increment).at[slot, :, glob_lat, glob_lon].add(weighted)
    members_adj = [lax.optimization_barrier(jnp.sum(ensemble[member].astype(jnp.float32) * back, axis=0)) for member in range(MEMBERS)]
    members_adj.append(0.5 * spread * lax.optimization_barrier(jnp.sum(back, axis=0)))
    adjoint = jnp.stack(members_adj)
    image = direction + smooth_field(vertical_adjoint(vertical, adjoint))
    norm_now = jnp.sum(residual * residual)
    alpha = norm_now / jnp.sum(direction * image)
    new_control = control + alpha * direction
    new_residual = residual - alpha * image
    norm_next = jnp.sum(new_residual * new_residual)
    new_direction = new_residual + norm_next / norm_now * direction
    return (new_control, new_residual, new_direction)
```

```python
import math

import jax
import jax.numpy as jnp
from jax import lax
from jax.experimental import pallas as pl
from jax.experimental.pallas import tpu as pltpu
from jax.sharding import PartitionSpec as P

LEV = 127
COMPS = 5
MEMBERS = 4
ROWS = 8
CELLS = 128
TILE = LEV * ROWS
LAT = 8
LON = 16
RECORDS = 256
CAP = 4
F32 = jnp.float32
BF16 = jnp.bfloat16


def filter_taps():
    raw = [math.exp(-(offset * offset) / 8.0) for offset in range(-3, 4)]
    scale = math.sqrt(sum(value * value for value in raw))
    return [value / scale for value in raw[3:]]


def iota(shape, dim):
    return lax.broadcasted_iota(jnp.int32, shape, dim)


def split(value):
    high = value.astype(BF16)
    return high, (value - high.astype(F32)).astype(BF16)


def mxu(a, b):
    return lax.dot_general(a, b, (((1,), (0,)), ((), ())), preferred_element_type=F32)


def level_matrix(matrix):
    high, low = split(matrix)
    return jnp.concatenate(
        [jnp.concatenate([high, high], 1), jnp.concatenate([low, jnp.zeros_like(low)], 1)], 0
    )


def lane_matrix(matrix):
    high, low = split(matrix)
    return jnp.concatenate(
        [jnp.concatenate([high, low], 1), jnp.concatenate([high, jnp.zeros_like(low)], 1)], 0
    )


def level_product(matrix, field):
    high, low = split(field)
    both = mxu(matrix, jnp.concatenate([high, low], 0))
    return both[:CELLS] + both[CELLS:]


def lane_product(field, matrix):
    high, low = split(field)
    both = mxu(jnp.concatenate([high, low], 1), matrix)
    return both[:, :CELLS] + both[:, CELLS:]


def kernel(
    live_ref, owner_ref, column_ref, slot_ref, corner_ref, weight_ref, std_ref, v_ref,
    d_hbm, r_hbm, ens_hbm,
    out_hbm, scalars_ref,
    d_nat, r_nat, o_nat, ens16, ens, x_ref, y_ref, halo, lon_out, lon_in, lon_lev, inc, dens,
    vpad, level_w, lane_w, rec_out1, rec_in1, rec_out2, rec_in2, rec_t, part1, part2,
    load_sem, lon_send, lon_recv, lat_send, lat_recv,
    rec1_send, rec1_recv, rec2_send, rec2_recv, red1_send, red1_recv, red2_send, red2_recv,
):
    lon = lax.axis_index("lon")
    lat = lax.axis_index("lat")
    taps = filter_taps()
    lane = iota((CELLS, CELLS), 1)

    def lat_peer(o):
        return lax.rem(lat + o, LAT)

    def lon_peer(o):
        return lax.rem(lon + o, LON)

    east, west = lon_peer(1), lon_peer(LON - 1)

    def remote(src, dst, send, recv, axis, peer):
        return pltpu.make_async_remote_copy(
            src_ref=src, dst_ref=dst, send_sem=send, recv_sem=recv,
            device_id={axis: peer}, device_id_type=pl.DeviceIdType.MESH,
        )

    barrier = pltpu.get_barrier_semaphore()

    @pl.loop(1, LAT)
    def _(o):
        pl.semaphore_signal(
            barrier, inc=1, device_id={"lat": lat_peer(o)}, device_id_type=pl.DeviceIdType.MESH
        )

    @pl.loop(1, LON)
    def _(o):
        pl.semaphore_signal(
            barrier, inc=1, device_id={"lon": lon_peer(o)}, device_id_type=pl.DeviceIdType.MESH
        )

    d_load = pltpu.make_async_copy(d_hbm, d_nat.at[pl.ds(0, COMPS * TILE)], load_sem.at[0])
    ens_load = pltpu.make_async_copy(ens_hbm, ens16, load_sem.at[1])
    r_load = pltpu.make_async_copy(r_hbm, r_nat.at[pl.ds(0, COMPS * TILE)], load_sem.at[2])
    d_load.start()
    ens_load.start()
    r_load.start()

    zeros8 = jnp.zeros((ROWS, CELLS), F32)
    d_nat[COMPS * TILE:, :] = zeros8
    r_nat[COMPS * TILE:, :] = zeros8
    ens[9 * TILE:, :] = zeros8
    vpad[...] = jnp.zeros((CELLS, CELLS), F32)
    vpad[0:LEV, 0:LEV] = v_ref[...]
    level_w[0] = level_matrix(vpad[...])
    level_w[1] = level_matrix(vpad[...].T)
    gap = jnp.abs(iota((CELLS, CELLS), 0) - lane)
    inner = jnp.zeros((CELLS, CELLS), F32)
    wrapped = inner
    for k in range(4):
        inner = jnp.where(gap == k, taps[k], inner)
        if k:
            wrapped = jnp.where(gap == CELLS - k, taps[k], wrapped)
    lane_w[0] = lane_matrix(inner)
    lane_w[1] = lane_matrix(wrapped)

    eye = iota((RECORDS, RECORDS), 0) == iota((RECORDS, RECORDS), 1)
    before = iota((RECORDS, RECORDS), 0) < iota((RECORDS, RECORDS), 1)
    owner = owner_ref[...]
    owner_col = jnp.sum(jnp.where(eye, owner, 0), axis=1, keepdims=True)
    rank = jnp.sum(jnp.where((owner_col == owner) & before, 1, 0), axis=0, keepdims=True)
    corner = corner_ref[...]
    place = (
        slot_ref[...] * (ROWS * CELLS) + column_ref[...]
        + corner[1:2] + CELLS * corner[2:3] + (CELLS + 1) * corner[3:4]
    )
    place_col = jnp.sum(jnp.where(eye, place, 0), axis=1, keepdims=True).astype(F32)
    target = (((owner & (LAT - 1)) * LON + (owner >> 3)) * CAP) + rank
    target = jnp.where(iota((1, RECORDS), 1) < live_ref[0], target, -1)
    chosen = jnp.where(iota((LAT * LON * CAP, RECORDS), 0) == target, 1.0, 0.0).astype(BF16)
    weights = jnp.concatenate([weight_ref[...], place_col], 1)
    high = weights.astype(BF16)
    mid = (weights - high.astype(F32)).astype(BF16)
    packed = mxu(chosen, jnp.concatenate([high, mid], 1))
    packed = packed[:, :CELLS] + packed[:, CELLS:]
    for s in range(LAT):
        rec_out1[s] = packed[s * LON * CAP:(s + 1) * LON * CAP]

    def blank(side):
        @pl.loop(0, 2 * COMPS)
        def _(n):
            halo[n, side] = jnp.zeros((3, CELLS, CELLS), F32)

    @pl.when(lat == 0)
    def _():
        blank(0)

    @pl.when(lat == LAT - 1)
    def _():
        blank(1)

    def d_rows(q):
        k, i = q // ROWS, lax.rem(q, ROWS)
        return d_nat[pl.ds(k * TILE + i, CELLS, stride=ROWS), :]

    def x_rows(q):
        return x_ref[q]

    def pack_lon(phase, rows):
        def body(q, carry):
            left, right = carry
            value = rows(q)
            here = (lane >= 3 * q) & (lane < 3 * q + 3)
            left = jnp.where(here, pltpu.roll(value, 3 * q + 3, 1), left)
            right = jnp.where(here, pltpu.roll(value, 3 * q, 1), right)
            return left, right

        zero = jnp.zeros((CELLS, CELLS), F32)
        left, right = lax.fori_loop(0, COMPS * ROWS, body, (zero, zero))
        lon_out[phase, 0] = left
        lon_out[phase, 1] = right

    def lon_copies(phase):
        return [
            remote(lon_out.at[phase, 0], lon_in.at[phase, 0], lon_send.at[phase, 0],
                   lon_recv.at[phase, 0], "lon", east),
            remote(lon_out.at[phase, 1], lon_in.at[phase, 1], lon_send.at[phase, 1],
                   lon_recv.at[phase, 1], "lon", west),
        ]

    def lat_north(phase, k):
        n = phase * COMPS + k
        return remote(y_ref.at[pl.ds(k * ROWS, 3)], halo.at[n, 1], lat_send.at[n, 1],
                      lat_recv.at[n, 1], "lat", lax.rem(lat + LAT - 1, LAT))

    def lat_south(phase, k):
        n = phase * COMPS + k
        return remote(y_ref.at[pl.ds(k * ROWS + 5, 3)], halo.at[n, 0], lat_send.at[n, 0],
                      lat_recv.at[n, 0], "lat", lax.rem(lat + 1, LAT))

    def lat_start(phase, k):
        @pl.when(lat > 0)
        def _():
            lat_north(phase, k).start()

        @pl.when(lat < LAT - 1)
        def _():
            lat_south(phase, k).start()

    def lat_arrived(phase, k):
        @pl.when(lat > 0)
        def _():
            lat_south(phase, k).wait_recv()

        @pl.when(lat < LAT - 1)
        def _():
            lat_north(phase, k).wait_recv()

    def lat_sent(phase):
        @pl.loop(0, COMPS)
        def _(k):
            @pl.when(lat > 0)
            def _():
                lat_north(phase, k).wait_send()

            @pl.when(lat < LAT - 1)
            def _():
                lat_south(phase, k).wait_send()

    def own_part(phase, rows):
        @pl.loop(0, COMPS * ROWS // 2)
        def _(p):
            value = jnp.concatenate([rows(2 * p), rows(2 * p + 1)], 1)
            value = level_product(level_w[phase], value)
            value = jnp.concatenate([value[:, :CELLS], value[:, CELLS:]], 0)
            value = lane_product(value, lane_w[0])
            y_ref[2 * p] = value[:CELLS]
            y_ref[2 * p + 1] = value[CELLS:]

    def lon_part(phase):
        for copy in lon_copies(phase):
            copy.wait_recv()
        edges = jnp.concatenate([lon_in[phase, 0], lon_in[phase, 1]], 1)
        edges = level_product(level_w[phase], edges)
        lon_lev[0] = edges[:, :CELLS]
        lon_lev[1] = edges[:, CELLS:]

        def spread(q):
            left = pltpu.roll(lon_lev[0], CELLS - 3 - 3 * q, 1)
            right = pltpu.roll(lon_lev[1], lax.rem(CELLS - 3 * q, CELLS), 1)
            return jnp.where(lane >= CELLS // 2, left, right)

        @pl.loop(0, COMPS)
        def _(k):
            @pl.loop(0, ROWS // 2)
            def _(p):
                q = k * ROWS + 2 * p
                value = lane_product(jnp.concatenate([spread(q), spread(q + 1)], 0), lane_w[1])
                y_ref[q] += value[:CELLS]
                y_ref[q + 1] += value[CELLS:]

            lat_start(phase, k)

    def lat_rows(phase, k, c):
        part = pl.ds(c * 8, 8)
        n = phase * COMPS + k
        rows = [halo[n, 0, j, part] for j in range(3)]
        rows += [y_ref[k * ROWS + i, part] for i in range(ROWS)]
        rows += [halo[n, 1, j, part] for j in range(3)]
        out = []
        for i in range(ROWS):
            total = taps[0] * rows[i + 3]
            for j in range(1, 4):
                total = total + taps[j] * (rows[i + 3 - j] + rows[i + 3 + j])
            out.append(total)
        return out

    def ens_rows(plane, c, i):
        return ens[pl.ds(plane * TILE + c * 64 + i, 8, stride=ROWS), :]

    def reduce_first(n, height, value):
        part1[n, lat, 0:height] = value

        @pl.loop(1, LAT)
        def _(o):
            ref = part1.at[n, lat, pl.ds(0, height)]
            remote(ref, ref, red1_send.at[n, o], red1_recv.at[n, lat], "lat", lat_peer(o)).start()

    def reduce_second(n, height):
        @pl.loop(1, LAT)
        def _(o):
            ref = part1.at[n, lat_peer(o), pl.ds(0, height)]
            remote(ref, ref, red1_send.at[n, o], red1_recv.at[n, lat_peer(o)], "lat",
                   lat_peer(o)).wait_recv()

        total = part1[n, 0, 0:height]
        for s in range(1, LAT):
            total = total + part1[n, s, 0:height]
        part2[n, lon, 0:height] = total

        @pl.loop(1, LON)
        def _(o):
            ref = part2.at[n, lon, pl.ds(0, height)]
            remote(ref, ref, red2_send.at[n, o], red2_recv.at[n, lon], "lon", lon_peer(o)).start()

    def reduce_last(n, height):
        @pl.loop(1, LON)
        def _(o):
            ref = part2.at[n, lon_peer(o), pl.ds(0, height)]
            remote(ref, ref, red2_send.at[n, o], red2_recv.at[n, lon_peer(o)], "lon",
                   lon_peer(o)).wait_recv()

        total = part2[n, 0, 0:height]
        for s in range(1, LON):
            total = total + part2[n, s, 0:height]
        return total

    def reduce_sent(n, height):
        @pl.loop(1, LAT)
        def _(o):
            ref = part1.at[n, lat, pl.ds(0, height)]
            remote(ref, ref, red1_send.at[n, o], red1_recv.at[n, lat], "lat",
                   lat_peer(o)).wait_send()

        @pl.loop(1, LON)
        def _(o):
            ref = part2.at[n, lon, pl.ds(0, height)]
            remote(ref, ref, red2_send.at[n, o], red2_recv.at[n, lon], "lon",
                   lon_peer(o)).wait_send()

    def rec1(o, slot):
        return remote(rec_out1.at[lat_peer(o)], rec_in1.at[slot], rec1_send.at[o],
                      rec1_recv.at[slot], "lat", lat_peer(o))

    def rec2(o, slot):
        return remote(rec_out2.at[lon_peer(o)], rec_in2.at[slot], rec2_send.at[o],
                      rec2_recv.at[slot], "lon", lon_peer(o))

    d_load.wait()
    pack_lon(0, d_rows)
    pl.semaphore_wait(barrier, LAT + LON - 2)
    for copy in lon_copies(0):
        copy.start()

    @pl.loop(1, LAT)
    def _(o):
        rec1(o, lat).start()

    rec_in1[lat] = rec_out1[lat]
    own_part(0, d_rows)
    lon_part(0)

    @pl.loop(1, LAT)
    def _(o):
        rec1(o, lat_peer(o)).wait_recv()

    @pl.loop(0, LON // 2)
    def _(p):
        rows = pl.ds(p * 2 * CAP, 2 * CAP)
        for s in range(LAT // 2):
            first, second = rec_in1[2 * s, rows], rec_in1[2 * s + 1, rows]
            rec_out2[2 * p, 8 * s:8 * s + 8] = jnp.concatenate([first[:CAP], second[:CAP]], 0)
            rec_out2[2 * p + 1, 8 * s:8 * s + 8] = jnp.concatenate([first[CAP:], second[CAP:]], 0)

    @pl.loop(1, LON)
    def _(o):
        rec2(o, lon).start()

    rec_in2[lon] = rec_out2[lon]

    ens_load.wait()

    @pl.loop(0, LEV)
    def _(n):
        ens[pl.ds(n * 64, 64), :] = ens16[pl.ds(n * 64, 64), :].astype(F32)

    ens[8 * TILE:9 * TILE, :] = 0.5 * std_ref[...].astype(F32)

    r_load.wait()

    def squares(n, carry):
        total_r, total_d = carry
        value_r = r_nat[pl.ds(n * 40, 40), :]
        value_d = d_nat[pl.ds(n * 40, 40), :]
        for s in range(5):
            piece = value_r[s * 8:s * 8 + 8]
            total_r = total_r + piece * piece
            piece = value_d[s * 8:s * 8 + 8]
            total_d = total_d + piece * piece
        return total_r, total_d

    sum_r, sum_d = lax.fori_loop(0, LEV, squares, (zeros8, zeros8))

    @pl.loop(1, LON)
    def _(o):
        rec2(o, lon_peer(o)).wait_recv()

    records = rec_in2[...].reshape(LAT * LON * CAP, CELLS)
    high, low = split(records.T)
    rec_t[...] = jnp.concatenate([high, low], 0)
    cell = records[:, LEV:].astype(jnp.int32)

    @pl.loop(0, ROWS)
    def _(p):
        hit = cell == iota((LAT * LON * CAP, 2 * CELLS), 1) + p * 2 * CELLS
        both = mxu(rec_t[...], jnp.where(hit, 1.0, 0.0).astype(BF16))
        total = both[:CELLS] + both[CELLS:]
        dens[2 * p] = total[:, :CELLS]
        dens[2 * p + 1] = total[:, CELLS:]

    @pl.loop(0, 2 * ROWS)
    def _(q):
        inc[q] = jnp.zeros((CELLS, CELLS), F32)

    @pl.loop(0, MEMBERS)
    def _(k):
        lat_arrived(0, k)

        @pl.loop(0, CELLS // 8)
        def _(c):
            rows = lat_rows(0, k, c)
            for t in range(2):
                for i in range(ROWS):
                    inc[t * ROWS + i, pl.ds(c * 8, 8)] += ens_rows(2 * k + t, c, i) * rows[i]

    lat_arrived(0, MEMBERS)

    def adjoint(c, curve):
        rows = lat_rows(0, MEMBERS, c)
        part = pl.ds(c * 8, 8)
        for i in range(ROWS):
            spread = ens_rows(8, c, i)
            static = spread * rows[i]
            inc0 = inc[i, part] + static
            inc1 = inc[ROWS + i, part] + static
            back0 = dens[i, part] * inc0
            back1 = dens[ROWS + i, part] * inc1
            curve = curve + back0 * inc0 + back1 * inc1
            for m in range(MEMBERS):
                x_ref[m * ROWS + i, part] = (
                    ens_rows(2 * m, c, i) * back0 + ens_rows(2 * m + 1, c, i) * back1
                )
            x_ref[MEMBERS * ROWS + i, part] = spread * (back0 + back1)
        return curve

    curve = lax.fori_loop(0, CELLS // 8, adjoint, sum_d)
    lat_sent(0)
    pack_lon(1, x_rows)
    for copy in lon_copies(1):
        copy.start()
    reduce_first(0, 16, jnp.concatenate([sum_r, curve], 0))
    own_part(1, x_rows)
    reduce_second(0, 16)
    lon_part(1)
    sums = reduce_last(0, 16)
    norm_now = jnp.sum(sums[:8], keepdims=True)
    alpha = norm_now / jnp.sum(sums[8:], keepdims=True)

    def out_copy(k):
        rows = pl.ds(k * TILE, TILE)
        return pltpu.make_async_copy(o_nat.at[rows], out_hbm.at[rows], load_sem.at[3 + k])

    def update(k, total):
        lat_arrived(1, k)

        def body(c, total):
            rows = lat_rows(1, k, c)
            real = iota((8, CELLS), 0) + c * 8 < LEV
            for i in range(ROWS):
                at = pl.ds(k * TILE + c * 64 + i, 8, stride=ROWS)
                value = r_nat[at, :] - alpha * (d_nat[at, :] + rows[i])
                o_nat[at, :] = value
                value = jnp.where(real, value, 0.0)
                total = total + value * value
            return total

        total = lax.fori_loop(0, CELLS // 8, body, total)
        out_copy(k).start()
        return total

    total = lax.fori_loop(0, COMPS, update, zeros8)
    reduce_first(1, 8, total)
    reduce_second(1, 8)
    norm_next = jnp.sum(reduce_last(1, 8), keepdims=True)
    first = iota((8, CELLS), 0) == 0
    scalars_ref[...] = jnp.where(first, alpha, norm_next / norm_now)

    @pl.loop(0, COMPS)
    def _(k):
        out_copy(k).wait()

    lat_sent(1)
    for phase in range(2):
        for copy in lon_copies(phase):
            copy.wait_send()
    reduce_sent(0, 16)
    reduce_sent(1, 8)

    @pl.loop(1, LAT)
    def _(o):
        rec1(o, lat).wait_send()

    @pl.loop(1, LON)
    def _(o):
        rec2(o, lon).wait_send()


def on_device(
    control, residual, direction, ensemble, static_std, vertical, owner, column, slot, corner,
    obs_weight, live_count,
):
    flat = (COMPS * TILE, CELLS)
    vmem = pl.BlockSpec(memory_space=pltpu.VMEM)
    hbm = pl.BlockSpec(memory_space=pl.ANY)
    dma = pltpu.SemaphoreType.DMA
    tail = (COMPS * TILE + ROWS, CELLS)
    square = (CELLS, CELLS)
    new_residual, scalars = pl.pallas_call(
        kernel,
        out_shape=(
            jax.ShapeDtypeStruct(flat, F32),
            jax.ShapeDtypeStruct((8, CELLS), F32),
        ),
        in_specs=[pl.BlockSpec(memory_space=pltpu.SMEM)] + [vmem] * 7 + [hbm] * 3,
        out_specs=(hbm, vmem),
        scratch_shapes=[
            pltpu.VMEM(tail, F32),
            pltpu.VMEM(tail, F32),
            pltpu.VMEM(tail, F32),
            pltpu.VMEM((8 * TILE, CELLS), BF16),
            pltpu.VMEM((9 * TILE + ROWS, CELLS), F32),
            pltpu.VMEM((COMPS * ROWS,) + square, F32),
            pltpu.VMEM((COMPS * ROWS,) + square, F32),
            pltpu.VMEM((2 * COMPS, 2, 3) + square, F32),
            pltpu.VMEM((2, 2) + square, F32),
            pltpu.VMEM((2, 2) + square, F32),
            pltpu.VMEM((2,) + square, F32),
            pltpu.VMEM((2 * ROWS,) + square, F32),
            pltpu.VMEM((2 * ROWS,) + square, F32),
            pltpu.VMEM(square, F32),
            pltpu.VMEM((2, 2 * CELLS, 2 * CELLS), BF16),
            pltpu.VMEM((2, 2 * CELLS, 2 * CELLS), BF16),
            pltpu.VMEM((LAT, LON * CAP, CELLS), F32),
            pltpu.VMEM((LAT, LON * CAP, CELLS), F32),
            pltpu.VMEM((LON, LAT * CAP, CELLS), F32),
            pltpu.VMEM((LON, LAT * CAP, CELLS), F32),
            pltpu.VMEM((2 * CELLS, LAT * LON * CAP), BF16),
            pltpu.VMEM((2, LAT, 16, CELLS), F32),
            pltpu.VMEM((2, LON, 16, CELLS), F32),
            dma((8,)),
            dma((2, 2)), dma((2, 2)),
            dma((2 * COMPS, 2)), dma((2 * COMPS, 2)),
            dma((LAT,)), dma((LAT,)),
            dma((LON,)), dma((LON,)),
            dma((2, LAT)), dma((2, LAT)),
            dma((2, LON)), dma((2, LON)),
        ],
        compiler_params=pltpu.CompilerParams(
            collective_id=0, has_side_effects=True, vmem_limit_bytes=40 * 1024 * 1024
        ),
        name="analysis_step",
    )(
        live_count,
        owner.reshape(1, RECORDS),
        column.reshape(1, RECORDS),
        slot.reshape(1, RECORDS),
        corner.T,
        obs_weight,
        static_std.reshape(TILE, CELLS),
        vertical,
        direction.reshape(flat),
        residual.reshape(flat),
        ensemble.reshape(8 * TILE, CELLS),
    )
    alpha, beta = scalars[0, 0], scalars[1, 0]
    new_residual = new_residual.reshape(residual.shape)
    return control + alpha * direction, new_residual, new_residual + beta * direction


def solution(mesh):
    field = P(None, None, "lat", "lon")
    return jax.shard_map(
        on_device,
        mesh=mesh,
        in_specs=(
            field,
            field,
            field,
            P(None, None, None, "lat", "lon"),
            P(None, "lat", "lon"),
            P(),
            P(("lon", "lat"), None),
            P(("lon", "lat")),
            P(("lon", "lat")),
            P(("lon", "lat"), None),
            P(("lon", "lat"), None),
            P(("lon", "lat")),
        ),
        out_specs=(field, field, field),
        check_vma=False,
    )
```

```python
import math

import jax
import jax.numpy as jnp
from jax import lax
from jax.experimental import pallas as pl
from jax.experimental.pallas import tpu as pltpu
from jax.sharding import PartitionSpec as P

LEV = 127
COMPS = 5
MEMBERS = 4
ROWS = 8
CELLS = 128
TILE = LEV * ROWS
LAT = 8
LON = 16
RECORDS = 256
CAP = 4
PAIRS = COMPS * ROWS // 2
F32 = jnp.float32
BF16 = jnp.bfloat16


def filter_taps():
    raw = [math.exp(-(offset * offset) / 8.0) for offset in range(-3, 4)]
    scale = math.sqrt(sum(value * value for value in raw))
    return [value / scale for value in raw[3:]]


def iota(shape, dim):
    return lax.broadcasted_iota(jnp.int32, shape, dim)


def split(value):
    high = value.astype(BF16)
    return high, (value - high.astype(F32)).astype(BF16)


def mxu(a, b):
    return lax.dot_general(a, b, (((1,), (0,)), ((), ())), preferred_element_type=F32)


def level_matrix(matrix):
    high, low = split(matrix)
    return jnp.concatenate(
        [jnp.concatenate([high, high], 1), jnp.concatenate([low, jnp.zeros_like(low)], 1)], 0
    )


def lane_matrix(matrix):
    high, low = split(matrix)
    return jnp.concatenate(
        [jnp.concatenate([high, low], 1), jnp.concatenate([high, jnp.zeros_like(low)], 1)], 0
    )


def level_product(matrix, field):
    high, low = split(field)
    both = mxu(matrix, jnp.concatenate([high, low], 0))
    return both[:CELLS] + both[CELLS:]


def lane_product(field, matrix):
    high, low = split(field)
    both = mxu(jnp.concatenate([high, low], 1), matrix)
    return both[:, :CELLS] + both[:, CELLS:]


def kernel(
    live_hbm, owner_hbm, column_hbm, slot_hbm, corner_hbm, weight_hbm, std_hbm, v_hbm,
    d_hbm, r_hbm, ens_hbm,
    out_hbm, scalars_ref,
    live_ref, owner_ref, column_ref, slot_ref, corner_ref, weight_ref, std_ref, v_ref,
    d_nat, r_nat, o_nat, ens16, ens, x_ref, y_ref, halo, lon_out, lon_in, inc, dens,
    vpad, level_w, lane_w, edge_w, pack_w, spread_w, rec_out1, rec_in1, rec_out2, rec_in2, rec_t,
    part1, part2,
    small_sem, load_sem, lon_send, lon_recv, lat_send, lat_recv,
    rec1_send, rec1_recv, rec2_send, rec2_recv, red1_send, red1_recv, red2_send, red2_recv,
):
    lon = lax.axis_index("lon")
    lat = lax.axis_index("lat")
    taps = filter_taps()
    lane = iota((CELLS, CELLS), 1)

    def lat_peer(o):
        return lax.rem(lat + o, LAT)

    def lon_peer(o):
        return lax.rem(lon + o, LON)

    east, west = lon_peer(1), lon_peer(LON - 1)

    def remote(src, dst, send, recv, axis, peer):
        return pltpu.make_async_remote_copy(
            src_ref=src, dst_ref=dst, send_sem=send, recv_sem=recv,
            device_id={axis: peer}, device_id_type=pl.DeviceIdType.MESH,
        )

    barrier = pltpu.get_barrier_semaphore()

    @pl.loop(1, LAT)
    def _(o):
        pl.semaphore_signal(
            barrier, inc=1, device_id={"lat": lat_peer(o)}, device_id_type=pl.DeviceIdType.MESH
        )

    @pl.loop(1, LON)
    def _(o):
        pl.semaphore_signal(
            barrier, inc=1, device_id={"lon": lon_peer(o)}, device_id_type=pl.DeviceIdType.MESH
        )

    d_load = pltpu.make_async_copy(d_hbm, d_nat.at[pl.ds(0, COMPS * TILE)], load_sem.at[0])
    ens_load = pltpu.make_async_copy(ens_hbm, ens16, load_sem.at[1])
    r_load = pltpu.make_async_copy(r_hbm, r_nat.at[pl.ds(0, COMPS * TILE)], load_sem.at[2])
    small_loads = [
        pltpu.make_async_copy(src, dst, small_sem.at[n])
        for n, (src, dst) in enumerate((
            (live_hbm, live_ref), (owner_hbm, owner_ref), (column_hbm, column_ref),
            (slot_hbm, slot_ref), (corner_hbm, corner_ref), (v_hbm, v_ref),
            (weight_hbm, weight_ref), (std_hbm, std_ref),
        ))
    ]
    for copy in small_loads:
        copy.start()
    d_load.start()
    ens_load.start()
    r_load.start()

    zeros8 = jnp.zeros((ROWS, CELLS), F32)
    d_nat[COMPS * TILE:, :] = zeros8
    r_nat[COMPS * TILE:, :] = zeros8
    ens[9 * TILE:, :] = zeros8
    vpad[...] = jnp.zeros((CELLS, CELLS), F32)

    high_dim, low_dim = iota((2 * CELLS, 2 * CELLS), 0), iota((2 * CELLS, 2 * CELLS), 1)

    def selection(cell, packed, first, last):
        column, half = cell & (CELLS - 1), cell >> 7
        where = jnp.where(
            (column >= CELLS - 3) & (packed >= last) & (packed < last + CELLS),
            packed - last - (column - (CELLS - 3)),
            jnp.where(
                (column < 3) & (packed >= first) & (packed < first + CELLS),
                packed - first - column, -1000,
            ),
        )
        return where - 3 * half

    to_pack = selection(high_dim, low_dim, CELLS, 0)
    to_cell = selection(low_dim, high_dim, 0, CELLS)

    @pl.loop(0, PAIRS)
    def _(p):
        pack_w[p] = jnp.where(to_pack == 6 * p, 1.0, 0.0).astype(BF16)
        spread_w[p] = jnp.where(to_cell == 6 * p, 1.0, 0.0).astype(BF16)

    third = ((high_dim & (CELLS - 1)) * 43691) >> 17
    same = (third == ((low_dim & (CELLS - 1)) * 43691) >> 17) & (high_dim >> 7 == low_dim >> 7)
    step = jnp.where(high_dim < CELLS, high_dim - low_dim, low_dim - high_dim)
    edge = jnp.zeros((2 * CELLS, 2 * CELLS), F32)
    for k in range(1, 4):
        edge = jnp.where(same & (step == 3 - k), taps[k], edge)
    edge_w[0], edge_w[1] = split(edge)

    for copy in small_loads:
        copy.wait()
    vpad[0:LEV, 0:LEV] = v_ref[...]
    level_w[0] = level_matrix(vpad[...])
    level_w[1] = level_matrix(vpad[...].T)
    gap = jnp.abs(iota((CELLS, CELLS), 0) - lane)
    inner = jnp.zeros((CELLS, CELLS), F32)
    for k in range(4):
        inner = jnp.where(gap == k, taps[k], inner)
    lane_w[...] = lane_matrix(inner)

    eye = iota((RECORDS, RECORDS), 0) == iota((RECORDS, RECORDS), 1)
    before = iota((RECORDS, RECORDS), 0) < iota((RECORDS, RECORDS), 1)
    owner = owner_ref[...]
    owner_col = jnp.sum(jnp.where(eye, owner, 0), axis=1, keepdims=True)
    rank = jnp.sum(jnp.where((owner_col == owner) & before, 1, 0), axis=0, keepdims=True)
    corner = corner_ref[...]
    place = (
        slot_ref[...] * (ROWS * CELLS) + column_ref[...]
        + corner[1:2] + CELLS * corner[2:3] + (CELLS + 1) * corner[3:4]
    )
    place_col = jnp.sum(jnp.where(eye, place, 0), axis=1, keepdims=True).astype(F32)
    target = (((owner & (LAT - 1)) * LON + (owner >> 3)) * CAP) + rank
    target = jnp.where(iota((1, RECORDS), 1) < live_ref[...], target, -1)
    chosen = jnp.where(iota((LAT * LON * CAP, RECORDS), 0) == target, 1.0, 0.0).astype(BF16)
    weights = jnp.concatenate([weight_ref[...], place_col], 1)
    high = weights.astype(BF16)
    mid = (weights - high.astype(F32)).astype(BF16)
    packed = mxu(chosen, jnp.concatenate([high, mid], 1))
    packed = packed[:, :CELLS] + packed[:, CELLS:]
    for s in range(LAT):
        rec_out1[s] = packed[s * LON * CAP:(s + 1) * LON * CAP]

    def blank(side):
        @pl.loop(0, 2 * COMPS)
        def _(n):
            halo[n, side] = jnp.zeros((3, CELLS, CELLS), F32)

    @pl.when(lat == 0)
    def _():
        blank(0)

    @pl.when(lat == LAT - 1)
    def _():
        blank(1)

    def d_rows(q):
        k, i = q // ROWS, q % ROWS
        return d_nat[pl.ds(k * TILE + i, CELLS, stride=ROWS), :]

    def x_rows(q):
        return x_ref[q]

    def pack_lon(phase, rows):
        total = None
        for k in range(COMPS):
            value = jnp.concatenate([rows(k * ROWS + i) for i in range(ROWS)], 1)
            high, low = split(value)
            weight = pack_w[4 * k:4 * k + 4].reshape(ROWS * CELLS, 2 * CELLS)
            part = mxu(jnp.concatenate([high, low], 0), weight)
            total = part if total is None else total + part
        total = total[:CELLS] + total[CELLS:]
        lon_out[phase, 0] = total[:, :CELLS]
        lon_out[phase, 1] = total[:, CELLS:]

    def lon_copies(phase):
        return [
            remote(lon_out.at[phase, 0], lon_in.at[phase, 0], lon_send.at[phase, 0],
                   lon_recv.at[phase, 0], "lon", east),
            remote(lon_out.at[phase, 1], lon_in.at[phase, 1], lon_send.at[phase, 1],
                   lon_recv.at[phase, 1], "lon", west),
        ]

    def lat_north(phase, k):
        n = phase * COMPS + k
        return remote(y_ref.at[pl.ds(k * ROWS, 3)], halo.at[n, 1], lat_send.at[n, 1],
                      lat_recv.at[n, 1], "lat", lax.rem(lat + LAT - 1, LAT))

    def lat_south(phase, k):
        n = phase * COMPS + k
        return remote(y_ref.at[pl.ds(k * ROWS + 5, 3)], halo.at[n, 0], lat_send.at[n, 0],
                      lat_recv.at[n, 0], "lat", lax.rem(lat + 1, LAT))

    def lat_start(phase, k):
        @pl.when(lat > 0)
        def _():
            lat_north(phase, k).start()

        @pl.when(lat < LAT - 1)
        def _():
            lat_south(phase, k).start()

    def lat_arrived(phase, k):
        @pl.when(lat > 0)
        def _():
            lat_south(phase, k).wait_recv()

        @pl.when(lat < LAT - 1)
        def _():
            lat_north(phase, k).wait_recv()

    def lat_sent(phase):
        @pl.loop(0, COMPS)
        def _(k):
            @pl.when(lat > 0)
            def _():
                lat_north(phase, k).wait_send()

            @pl.when(lat < LAT - 1)
            def _():
                lat_south(phase, k).wait_send()

    def own_part(phase, rows):
        for k in range(COMPS):
            value = jnp.concatenate([rows(k * ROWS + i) for i in range(ROWS)], 1)
            value = level_product(level_w[phase], value)
            value = jnp.concatenate(
                [value[:, i * CELLS:(i + 1) * CELLS] for i in range(ROWS)], 0
            )
            value = lane_product(value, lane_w[...])
            for i in range(ROWS):
                y_ref[k * ROWS + i] = value[i * CELLS:(i + 1) * CELLS]

    def lon_part(phase):
        for copy in lon_copies(phase):
            copy.wait_recv()
        edges = jnp.concatenate([lon_in[phase, 0], lon_in[phase, 1]], 1)
        high, low = split(level_product(level_w[phase], edges))
        both = mxu(jnp.concatenate([high, low], 0), edge_w[0])
        edges = both[:CELLS] + both[CELLS:] + mxu(high, edge_w[1])
        high, low = split(edges)
        edges = jnp.concatenate([high, low], 0)
        for k in range(COMPS):
            for p in range(4 * k, 4 * k + 4):
                both = mxu(edges, spread_w[p])
                both = both[:CELLS] + both[CELLS:]
                y_ref[2 * p] += both[:, :CELLS]
                y_ref[2 * p + 1] += both[:, CELLS:]
            lat_start(phase, k)

    def lat_rows(phase, k, c):
        part = pl.ds(c * 8, 8)
        n = phase * COMPS + k
        rows = [halo[n, 0, j, part] for j in range(3)]
        rows += [y_ref[k * ROWS + i, part] for i in range(ROWS)]
        rows += [halo[n, 1, j, part] for j in range(3)]
        out = []
        for i in range(ROWS):
            total = taps[0] * rows[i + 3]
            for j in range(1, 4):
                total = total + taps[j] * (rows[i + 3 - j] + rows[i + 3 + j])
            out.append(total)
        return out

    def ens_rows(plane, c, i):
        return ens[pl.ds(plane * TILE + c * 64 + i, 8, stride=ROWS), :]

    def reduce_first(n, height, value):
        part1[n, lat, 0:height] = value

        @pl.loop(1, LAT)
        def _(o):
            ref = part1.at[n, lat, pl.ds(0, height)]
            remote(ref, ref, red1_send.at[n, o], red1_recv.at[n, lat], "lat", lat_peer(o)).start()

    def reduce_second(n, height):
        @pl.loop(1, LAT)
        def _(o):
            ref = part1.at[n, lat_peer(o), pl.ds(0, height)]
            remote(ref, ref, red1_send.at[n, o], red1_recv.at[n, lat_peer(o)], "lat",
                   lat_peer(o)).wait_recv()

        total = part1[n, 0, 0:height]
        for s in range(1, LAT):
            total = total + part1[n, s, 0:height]
        part2[n, lon, 0:height] = total

        @pl.loop(1, LON)
        def _(o):
            ref = part2.at[n, lon, pl.ds(0, height)]
            remote(ref, ref, red2_send.at[n, o], red2_recv.at[n, lon], "lon", lon_peer(o)).start()

    def reduce_last(n, height):
        @pl.loop(1, LON)
        def _(o):
            ref = part2.at[n, lon_peer(o), pl.ds(0, height)]
            remote(ref, ref, red2_send.at[n, o], red2_recv.at[n, lon_peer(o)], "lon",
                   lon_peer(o)).wait_recv()

        total = part2[n, 0, 0:height]
        for s in range(1, LON):
            total = total + part2[n, s, 0:height]
        return total

    def reduce_sent(n, height):
        @pl.loop(1, LAT)
        def _(o):
            ref = part1.at[n, lat, pl.ds(0, height)]
            remote(ref, ref, red1_send.at[n, o], red1_recv.at[n, lat], "lat",
                   lat_peer(o)).wait_send()

        @pl.loop(1, LON)
        def _(o):
            ref = part2.at[n, lon, pl.ds(0, height)]
            remote(ref, ref, red2_send.at[n, o], red2_recv.at[n, lon], "lon",
                   lon_peer(o)).wait_send()

    def rec1(o, slot):
        return remote(rec_out1.at[lat_peer(o)], rec_in1.at[slot], rec1_send.at[o],
                      rec1_recv.at[slot], "lat", lat_peer(o))

    def rec2(o, slot):
        return remote(rec_out2.at[lon_peer(o)], rec_in2.at[slot], rec2_send.at[o],
                      rec2_recv.at[slot], "lon", lon_peer(o))

    d_load.wait()
    pack_lon(0, d_rows)
    pl.semaphore_wait(barrier, LAT + LON - 2)
    for copy in lon_copies(0):
        copy.start()

    @pl.loop(1, LAT)
    def _(o):
        rec1(o, lat).start()

    rec_in1[lat] = rec_out1[lat]
    own_part(0, d_rows)
    lon_part(0)

    @pl.loop(1, LAT)
    def _(o):
        rec1(o, lat_peer(o)).wait_recv()

    @pl.loop(0, LON // 2)
    def _(p):
        rows = pl.ds(p * 2 * CAP, 2 * CAP)
        for s in range(LAT // 2):
            first, second = rec_in1[2 * s, rows], rec_in1[2 * s + 1, rows]
            rec_out2[2 * p, 8 * s:8 * s + 8] = jnp.concatenate([first[:CAP], second[:CAP]], 0)
            rec_out2[2 * p + 1, 8 * s:8 * s + 8] = jnp.concatenate([first[CAP:], second[CAP:]], 0)

    @pl.loop(1, LON)
    def _(o):
        rec2(o, lon).start()

    rec_in2[lon] = rec_out2[lon]

    ens_load.wait()

    @pl.loop(0, LEV)
    def _(n):
        ens[pl.ds(n * 64, 64), :] = ens16[pl.ds(n * 64, 64), :].astype(F32)

    ens[8 * TILE:9 * TILE, :] = 0.5 * std_ref[...].astype(F32)

    r_load.wait()

    def squares(n, carry):
        total_r, total_d = carry
        value_r = r_nat[pl.ds(n * 40, 40), :]
        value_d = d_nat[pl.ds(n * 40, 40), :]
        for s in range(5):
            piece = value_r[s * 8:s * 8 + 8]
            total_r = total_r + piece * piece
            piece = value_d[s * 8:s * 8 + 8]
            total_d = total_d + piece * piece
        return total_r, total_d

    sum_r, sum_d = lax.fori_loop(0, LEV, squares, (zeros8, zeros8))

    @pl.loop(1, LON)
    def _(o):
        rec2(o, lon_peer(o)).wait_recv()

    records = rec_in2[...].reshape(LAT * LON * CAP, CELLS)
    high, low = split(records.T)
    rec_t[...] = jnp.concatenate([high, low], 0)
    cell = records[:, LEV:].astype(jnp.int32)

    @pl.loop(0, ROWS)
    def _(p):
        hit = cell == iota((LAT * LON * CAP, 2 * CELLS), 1) + p * 2 * CELLS
        both = mxu(rec_t[...], jnp.where(hit, 1.0, 0.0).astype(BF16))
        total = both[:CELLS] + both[CELLS:]
        dens[2 * p] = total[:, :CELLS]
        dens[2 * p + 1] = total[:, CELLS:]

    @pl.loop(0, 2 * ROWS)
    def _(q):
        inc[q] = jnp.zeros((CELLS, CELLS), F32)

    @pl.loop(0, MEMBERS)
    def _(k):
        lat_arrived(0, k)

        @pl.loop(0, CELLS // 8)
        def _(c):
            rows = lat_rows(0, k, c)
            for t in range(2):
                for i in range(ROWS):
                    inc[t * ROWS + i, pl.ds(c * 8, 8)] += ens_rows(2 * k + t, c, i) * rows[i]

    lat_arrived(0, MEMBERS)

    def adjoint(c, curve):
        rows = lat_rows(0, MEMBERS, c)
        part = pl.ds(c * 8, 8)
        for i in range(ROWS):
            spread = ens_rows(8, c, i)
            static = spread * rows[i]
            inc0 = inc[i, part] + static
            inc1 = inc[ROWS + i, part] + static
            back0 = dens[i, part] * inc0
            back1 = dens[ROWS + i, part] * inc1
            curve = curve + back0 * inc0 + back1 * inc1
            for m in range(MEMBERS):
                x_ref[m * ROWS + i, part] = (
                    ens_rows(2 * m, c, i) * back0 + ens_rows(2 * m + 1, c, i) * back1
                )
            x_ref[MEMBERS * ROWS + i, part] = spread * (back0 + back1)
        return curve

    curve = lax.fori_loop(0, CELLS // 8, adjoint, sum_d)
    lat_sent(0)
    pack_lon(1, x_rows)
    for copy in lon_copies(1):
        copy.start()
    reduce_first(0, 16, jnp.concatenate([sum_r, curve], 0))
    own_part(1, x_rows)
    reduce_second(0, 16)
    lon_part(1)
    sums = reduce_last(0, 16)
    norm_now = jnp.sum(sums[:8], keepdims=True)
    alpha = norm_now / jnp.sum(sums[8:], keepdims=True)

    def out_copy(k):
        rows = pl.ds(k * TILE, TILE)
        return pltpu.make_async_copy(o_nat.at[rows], out_hbm.at[rows], load_sem.at[3 + k])

    def update(k, total):
        lat_arrived(1, k)

        def body(c, total):
            rows = lat_rows(1, k, c)
            real = iota((8, CELLS), 0) + c * 8 < LEV
            for i in range(ROWS):
                at = pl.ds(k * TILE + c * 64 + i, 8, stride=ROWS)
                value = r_nat[at, :] - alpha * (d_nat[at, :] + rows[i])
                o_nat[at, :] = value
                value = jnp.where(real, value, 0.0)
                total = total + value * value
            return total

        total = lax.fori_loop(0, CELLS // 8, body, total)
        out_copy(k).start()
        return total

    total = lax.fori_loop(0, COMPS, update, zeros8)
    reduce_first(1, 8, total)
    reduce_second(1, 8)
    norm_next = jnp.sum(reduce_last(1, 8), keepdims=True)
    first = iota((8, CELLS), 0) == 0
    scalars_ref[...] = jnp.where(first, alpha, norm_next / norm_now)

    @pl.loop(0, COMPS)
    def _(k):
        out_copy(k).wait()

    lat_sent(1)
    for phase in range(2):
        for copy in lon_copies(phase):
            copy.wait_send()
    reduce_sent(0, 16)
    reduce_sent(1, 8)

    @pl.loop(1, LAT)
    def _(o):
        rec1(o, lat).wait_send()

    @pl.loop(1, LON)
    def _(o):
        rec2(o, lon).wait_send()


def on_device(
    control, residual, direction, ensemble, static_std, vertical, owner, column, slot, corner,
    obs_weight, live_count,
):
    flat = (COMPS * TILE, CELLS)
    vmem = pl.BlockSpec(memory_space=pltpu.VMEM)
    hbm = pl.BlockSpec(memory_space=pltpu.HBM)
    dma = pltpu.SemaphoreType.DMA
    tail = (COMPS * TILE + ROWS, CELLS)
    square = (CELLS, CELLS)
    new_residual, scalars = pl.pallas_call(
        kernel,
        out_shape=(
            jax.ShapeDtypeStruct(flat, F32),
            jax.ShapeDtypeStruct((8, CELLS), F32),
        ),
        in_specs=[hbm] * 11,
        out_specs=(hbm, vmem),
        scratch_shapes=[
            pltpu.VMEM((1, 1), jnp.int32),
            pltpu.VMEM((1, RECORDS), jnp.int32),
            pltpu.VMEM((1, RECORDS), jnp.int32),
            pltpu.VMEM((1, RECORDS), jnp.int32),
            pltpu.VMEM((4, RECORDS), jnp.int32),
            pltpu.VMEM((RECORDS, LEV), F32),
            pltpu.VMEM((TILE, CELLS), BF16),
            pltpu.VMEM((LEV, LEV), F32),
            pltpu.VMEM(tail, F32),
            pltpu.VMEM(tail, F32),
            pltpu.VMEM(tail, F32),
            pltpu.VMEM((8 * TILE, CELLS), BF16),
            pltpu.VMEM((9 * TILE + ROWS, CELLS), F32),
            pltpu.VMEM((COMPS * ROWS,) + square, F32),
            pltpu.VMEM((COMPS * ROWS,) + square, F32),
            pltpu.VMEM((2 * COMPS, 2, 3) + square, F32),
            pltpu.VMEM((2, 2) + square, F32),
            pltpu.VMEM((2, 2) + square, F32),
            pltpu.VMEM((2 * ROWS,) + square, F32),
            pltpu.VMEM((2 * ROWS,) + square, F32),
            pltpu.VMEM(square, F32),
            pltpu.VMEM((2, 2 * CELLS, 2 * CELLS), BF16),
            pltpu.VMEM((2 * CELLS, 2 * CELLS), BF16),
            pltpu.VMEM((2, 2 * CELLS, 2 * CELLS), BF16),
            pltpu.VMEM((PAIRS, 2 * CELLS, 2 * CELLS), BF16),
            pltpu.VMEM((PAIRS, 2 * CELLS, 2 * CELLS), BF16),
            pltpu.VMEM((LAT, LON * CAP, CELLS), F32),
            pltpu.VMEM((LAT, LON * CAP, CELLS), F32),
            pltpu.VMEM((LON, LAT * CAP, CELLS), F32),
            pltpu.VMEM((LON, LAT * CAP, CELLS), F32),
            pltpu.VMEM((2 * CELLS, LAT * LON * CAP), BF16),
            pltpu.VMEM((2, LAT, 16, CELLS), F32),
            pltpu.VMEM((2, LON, 16, CELLS), F32),
            dma((8,)),
            dma((8,)),
            dma((2, 2)), dma((2, 2)),
            dma((2 * COMPS, 2)), dma((2 * COMPS, 2)),
            dma((LAT,)), dma((LAT,)),
            dma((LON,)), dma((LON,)),
            dma((2, LAT)), dma((2, LAT)),
            dma((2, LON)), dma((2, LON)),
        ],
        compiler_params=pltpu.CompilerParams(
            collective_id=0, has_side_effects=True, vmem_limit_bytes=60 * 1024 * 1024
        ),
        name="analysis_step",
    )(
        live_count.reshape(1, 1),
        owner.reshape(1, RECORDS),
        column.reshape(1, RECORDS),
        slot.reshape(1, RECORDS),
        corner.T,
        obs_weight,
        static_std.reshape(TILE, CELLS),
        vertical,
        direction.reshape(flat),
        residual.reshape(flat),
        ensemble.reshape(8 * TILE, CELLS),
    )
    alpha, beta = scalars[0, 0], scalars[1, 0]
    new_residual = new_residual.reshape(residual.shape)
    return control + alpha * direction, new_residual, new_residual + beta * direction


def solution(mesh):
    field = P(None, None, "lat", "lon")
    return jax.shard_map(
        on_device,
        mesh=mesh,
        in_specs=(
            field,
            field,
            field,
            P(None, None, None, "lat", "lon"),
            P(None, "lat", "lon"),
            P(),
            P(("lon", "lat"), None),
            P(("lon", "lat")),
            P(("lon", "lat")),
            P(("lon", "lat"), None),
            P(("lon", "lat"), None),
            P(("lon", "lat")),
        ),
        out_specs=(field, field, field),
        check_vma=False,
    )
```

```python
import math

import jax
import jax.numpy as jnp
from jax import lax
from jax.experimental import pallas as pl
from jax.experimental.pallas import tpu as pltpu
from jax.sharding import PartitionSpec as P

LEV = 127
COMPS = 5
MEMBERS = 4
ROWS = 8
CELLS = 128
TILE = LEV * ROWS
LAT = 8
LON = 16
RECORDS = 256
CAP = 4
PAIRS = COMPS * ROWS // 2
PACKED = [(q % COMPS) * ROWS + q // COMPS for q in range(COMPS * ROWS)]
EDGE = 3 * 3 * COMPS
F32 = jnp.float32
BF16 = jnp.bfloat16


def filter_taps():
    raw = [math.exp(-(offset * offset) / 8.0) for offset in range(-3, 4)]
    scale = math.sqrt(sum(value * value for value in raw))
    return [value / scale for value in raw[3:]]


def iota(shape, dim):
    return lax.broadcasted_iota(jnp.int32, shape, dim)


def split(value):
    high = value.astype(BF16)
    return high, (value - high.astype(F32)).astype(BF16)


def mxu(a, b):
    return lax.dot_general(a, b, (((1,), (0,)), ((), ())), preferred_element_type=F32)


def level_matrix(matrix):
    high, low = split(matrix)
    return jnp.concatenate(
        [jnp.concatenate([high, high], 1), jnp.concatenate([low, jnp.zeros_like(low)], 1)], 0
    )


def lane_matrix(matrix):
    high, low = split(matrix)
    return jnp.concatenate(
        [jnp.concatenate([high, low], 1), jnp.concatenate([high, jnp.zeros_like(low)], 1)], 0
    )


def level_product(matrix, field):
    high, low = split(field)
    both = mxu(matrix, jnp.concatenate([high, low], 0))
    return both[:CELLS] + both[CELLS:]


def lane_product(field, matrix):
    high, low = split(field)
    both = mxu(jnp.concatenate([high, low], 1), matrix)
    return both[:, :CELLS] + both[:, CELLS:]


def kernel(
    live_hbm, owner_hbm, column_hbm, slot_hbm, corner_hbm, weight_hbm, std_hbm, v_hbm,
    d_hbm, r_hbm, ens_hbm, c_hbm,
    control_ref, residual_ref, direction_ref,
    live_ref, owner_ref, column_ref, slot_ref, corner_ref, weight_ref, std_ref, v_ref,
    d_nat, r_nat, c_nat, ens16, ens, x_ref, y_ref, z_ref, halo, corner_rows, lon_out, lon_in,
    corner_out, corner_in, inc, dens,
    vpad, level_w, lane_w, edge_w, pack_w, spread_w, corner_w, rec_out1, rec_in1, rec_out2, rec_in2, rec_t,
    part1, part2,
    small_sem, d_sem, load_sem, lon_send, lon_recv, corner_send, corner_recv, lat_send, lat_recv,
    rec1_send, rec1_recv, rec2_send, rec2_recv, red1_send, red1_recv, red2_send, red2_recv,
):
    lon = lax.axis_index("lon")
    lat = lax.axis_index("lat")
    taps = filter_taps()
    lane = iota((CELLS, CELLS), 1)

    def lat_peer(o):
        return lax.rem(lat + o, LAT)

    def lon_peer(o):
        return lax.rem(lon + o, LON)

    east, west = lon_peer(1), lon_peer(LON - 1)

    def remote(src, dst, send, recv, axis, peer):
        return pltpu.make_async_remote_copy(
            src_ref=src, dst_ref=dst, send_sem=send, recv_sem=recv,
            device_id={axis: peer}, device_id_type=pl.DeviceIdType.MESH,
        )

    barrier = pltpu.get_barrier_semaphore()

    @pl.loop(1, LAT)
    def _(o):
        pl.semaphore_signal(
            barrier, inc=1, device_id={"lat": lat_peer(o)}, device_id_type=pl.DeviceIdType.MESH
        )

    @pl.loop(1, LON)
    def _(o):
        pl.semaphore_signal(
            barrier, inc=1, device_id={"lon": lon_peer(o)}, device_id_type=pl.DeviceIdType.MESH
        )

    d_loads = [
        pltpu.make_async_copy(
            d_hbm.at[pl.ds(k * TILE, TILE)], d_nat.at[pl.ds(k * TILE, TILE)], d_sem.at[k]
        )
        for k in range(COMPS)
    ]
    ens_load = pltpu.make_async_copy(ens_hbm, ens16, load_sem.at[0])
    r_load = pltpu.make_async_copy(r_hbm, r_nat.at[pl.ds(0, COMPS * TILE)], load_sem.at[1])
    c_load = pltpu.make_async_copy(c_hbm, c_nat, load_sem.at[2])
    small_loads = [
        pltpu.make_async_copy(src, dst, small_sem.at[n])
        for n, (src, dst) in enumerate((
            (live_hbm, live_ref), (owner_hbm, owner_ref), (column_hbm, column_ref),
            (slot_hbm, slot_ref), (corner_hbm, corner_ref), (v_hbm, v_ref),
            (weight_hbm, weight_ref), (std_hbm, std_ref),
        ))
    ]
    small_loads[5].start()
    for copy in d_loads:
        copy.start()
    for n, copy in enumerate(small_loads):
        if n != 5:
            copy.start()
    ens_load.start()
    r_load.start()
    c_load.start()

    zeros8 = jnp.zeros((ROWS, CELLS), F32)
    d_nat[COMPS * TILE:, :] = zeros8
    r_nat[COMPS * TILE:, :] = zeros8
    ens[9 * TILE:, :] = zeros8
    vpad[...] = jnp.zeros((CELLS, CELLS), F32)

    small_loads[5].wait()
    vpad[0:LEV, 0:LEV] = v_ref[...]
    level_w[0] = level_matrix(vpad[...])
    level_w[1] = level_matrix(vpad[...].T)
    gap = jnp.abs(iota((CELLS, CELLS), 0) - lane)
    inner = jnp.zeros((CELLS, CELLS), F32)
    for k in range(4):
        inner = jnp.where(gap == k, taps[k], inner)
    lane_w[...] = lane_matrix(inner)

    def build_selections():
        part = iota((2 * CELLS, 2 * CELLS), 0) & (CELLS - 1)
        cells = iota((2 * CELLS, 2 * CELLS), 1)
        column = cells & (CELLS - 1)
        wanted = jnp.where(
            (column < 3) & (part < CELLS // 2), part - column,
            jnp.where(
                (column >= CELLS - 3) & (part >= CELLS // 2),
                part - CELLS // 2 - (column - (CELLS - 3)), -1000,
            ),
        ) - 3 * (cells >> 7)

        @pl.loop(0, 8)
        def _(p):
            corner_w[p] = jnp.where(wanted == 6 * p, 1.0, 0.0).astype(BF16)

        high_dim, low_dim = iota((2 * CELLS, 2 * CELLS), 0), iota((2 * CELLS, 2 * CELLS), 1)

        def selection(cell, packed, first, last):
            column, half = cell & (CELLS - 1), cell >> 7
            where = jnp.where(
                (column >= CELLS - 3) & (packed >= last) & (packed < last + CELLS),
                packed - last - (column - (CELLS - 3)),
                jnp.where(
                    (column < 3) & (packed >= first) & (packed < first + CELLS),
                    packed - first - column, -1000,
                ),
            )
            return where - 3 * half

        to_pack = selection(high_dim, low_dim, CELLS, 0)
        to_cell = selection(low_dim, high_dim, 0, CELLS)

        @pl.loop(0, PAIRS)
        def _(p):
            pack_w[p] = jnp.where(to_pack == 6 * p, 1.0, 0.0).astype(BF16)
            spread_w[p] = jnp.where(to_cell == 6 * p, 1.0, 0.0).astype(BF16)

        third = ((high_dim & (CELLS - 1)) * 43691) >> 17
        same = (third == ((low_dim & (CELLS - 1)) * 43691) >> 17) & (high_dim >> 7 == low_dim >> 7)
        step = jnp.where(high_dim < CELLS, high_dim - low_dim, low_dim - high_dim)
        edge = jnp.zeros((2 * CELLS, 2 * CELLS), F32)
        for k in range(1, 4):
            edge = jnp.where(same & (step == 3 - k), taps[k], edge)
        edge_w[0], edge_w[1] = split(edge)

    def pack_records():
        for n, copy in enumerate(small_loads):
            if n != 5:
                copy.wait()
        eye = iota((RECORDS, RECORDS), 0) == iota((RECORDS, RECORDS), 1)
        before = iota((RECORDS, RECORDS), 0) < iota((RECORDS, RECORDS), 1)
        owner = owner_ref[...]
        owner_col = jnp.sum(jnp.where(eye, owner, 0), axis=1, keepdims=True)
        rank = jnp.sum(jnp.where((owner_col == owner) & before, 1, 0), axis=0, keepdims=True)
        corner = corner_ref[...]
        place = (
            slot_ref[...] * (ROWS * CELLS) + column_ref[...]
            + corner[1:2] + CELLS * corner[2:3] + (CELLS + 1) * corner[3:4]
        )
        place_col = jnp.sum(jnp.where(eye, place, 0), axis=1, keepdims=True).astype(F32)
        target = (((owner & (LAT - 1)) * LON + (owner >> 3)) * CAP) + rank
        target = jnp.where(iota((1, RECORDS), 1) < live_ref[...], target, -1)
        chosen = jnp.where(iota((LAT * LON * CAP, RECORDS), 0) == target, 1.0, 0.0).astype(BF16)
        weights = jnp.concatenate([weight_ref[...], place_col], 1)
        high = weights.astype(BF16)
        mid = (weights - high.astype(F32)).astype(BF16)
        packed = mxu(chosen, jnp.concatenate([high, mid], 1))
        packed = packed[:, :CELLS] + packed[:, CELLS:]
        for s in range(LAT):
            rec_out1[s] = packed[s * LON * CAP:(s + 1) * LON * CAP]

    def blank(side):
        @pl.loop(0, 2 * COMPS)
        def _(n):
            halo[n, side] = jnp.zeros((3, CELLS, CELLS), F32)

        @pl.loop(0, COMPS)
        def _(k):
            corner_rows[k, side] = jnp.zeros((3, CELLS, CELLS), F32)

    @pl.when(lat == 0)
    def _():
        blank(0)

    @pl.when(lat == LAT - 1)
    def _():
        blank(1)

    def d_rows(q):
        k, i = q // ROWS, q % ROWS
        return d_nat[pl.ds(k * TILE + i, CELLS, stride=ROWS), :]

    def x_rows(q):
        return x_ref[q]

    def pack_lon(phase, rows):
        total = None
        for k in range(COMPS):
            value = jnp.concatenate([rows(PACKED[k * ROWS + i]) for i in range(ROWS)], 1)
            high, low = split(value)
            weight = pack_w[4 * k:4 * k + 4].reshape(ROWS * CELLS, 2 * CELLS)
            part = mxu(jnp.concatenate([high, low], 0), weight)
            total = part if total is None else total + part
        total = total[:CELLS] + total[CELLS:]
        lon_out[phase, 0] = total[:, :CELLS]
        lon_out[phase, 1] = total[:, CELLS:]

    def edge_copies(phase):
        return [
            remote(lon_out.at[phase, side], lon_in.at[phase, side], lon_send.at[phase, side],
                   lon_recv.at[phase, side], "lon", (east, west)[side])
            for side in range(2)
        ]

    def corner_north(phase):
        return remote(corner_out.at[phase, 0], corner_in.at[phase, 1], corner_send.at[phase, 1],
                      corner_recv.at[phase, 1], "lat", lax.rem(lat + LAT - 1, LAT))

    def corner_south(phase):
        return remote(corner_out.at[phase, 1], corner_in.at[phase, 0], corner_send.at[phase, 0],
                      corner_recv.at[phase, 0], "lat", lax.rem(lat + 1, LAT))

    def lat_north(phase, k):
        n = phase * COMPS + k
        return remote(y_ref.at[pl.ds(k * ROWS, 3)], halo.at[n, 1], lat_send.at[n, 1],
                      lat_recv.at[n, 1], "lat", lax.rem(lat + LAT - 1, LAT))

    def lat_south(phase, k):
        n = phase * COMPS + k
        return remote(y_ref.at[pl.ds(k * ROWS + 5, 3)], halo.at[n, 0], lat_send.at[n, 0],
                      lat_recv.at[n, 0], "lat", lax.rem(lat + 1, LAT))

    def lat_start(phase, k):
        @pl.when(lat > 0)
        def _():
            lat_north(phase, k).start()

        @pl.when(lat < LAT - 1)
        def _():
            lat_south(phase, k).start()

    def lat_arrived(phase, k):
        @pl.when(lat > 0)
        def _():
            lat_south(phase, k).wait_recv()

        @pl.when(lat < LAT - 1)
        def _():
            lat_north(phase, k).wait_recv()

    def lat_sent(phase):
        @pl.loop(0, COMPS)
        def _(k):
            @pl.when(lat > 0)
            def _():
                lat_north(phase, k).wait_send()

            @pl.when(lat < LAT - 1)
            def _():
                lat_south(phase, k).wait_send()

    def own_part(phase, k, rows):
        value = jnp.concatenate([rows(k * ROWS + i) for i in range(ROWS)], 1)
        value = level_product(level_w[phase], value)
        value = jnp.concatenate([value[:, i * CELLS:(i + 1) * CELLS] for i in range(ROWS)], 0)
        value = lane_product(value, lane_w[...])
        for i in range(ROWS):
            y_ref[k * ROWS + i] = value[i * CELLS:(i + 1) * CELLS]

    def lon_part(phase):
        for copy in edge_copies(phase):
            copy.wait_recv()
        edges = jnp.concatenate([lon_in[phase, 0], lon_in[phase, 1]], 1)
        high, low = split(level_product(level_w[phase], edges))
        both = mxu(jnp.concatenate([high, low], 0), edge_w[0])
        edges = both[:CELLS] + both[CELLS:] + mxu(high, edge_w[1])
        left, right = edges[:, :CELLS], edges[:, CELLS:]
        half = CELLS // 2
        corner_out[phase, 0] = jnp.where(lane < half, left, pltpu.roll(right, half, 1))
        start = COMPS * ROWS * 3 - EDGE
        corner_out[phase, 1] = jnp.where(
            lane < half, pltpu.roll(left, CELLS - start, 1),
            pltpu.roll(right, CELLS + half - start, 1),
        )

        @pl.when(lat > 0)
        def _():
            corner_north(phase).start()

        @pl.when(lat < LAT - 1)
        def _():
            corner_south(phase).start()

        high, low = split(edges)
        edges = jnp.concatenate([high, low], 0)
        for p in range(PAIRS):
            both = mxu(edges, spread_w[p])
            both = both[:CELLS] + both[CELLS:]
            for n in range(2):
                q = PACKED[2 * p + n]
                z_ref[q] = y_ref[q] + both[:, n * CELLS:(n + 1) * CELLS]

    def corner_part(phase):
        def fill(side):
            high, low = split(corner_in[phase, side])
            edges = jnp.concatenate([high, low], 1)
            for p in range(8):
                both = mxu(edges, corner_w[p])
                for n in range(2):
                    q = 2 * p + n
                    if q < 3 * COMPS:
                        corner_rows[q % COMPS, side, q // COMPS] = (
                            both[:, n * CELLS:(n + 1) * CELLS]
                        )

        @pl.when(lat > 0)
        def _():
            corner_south(phase).wait_recv()
            fill(0)

        @pl.when(lat < LAT - 1)
        def _():
            corner_north(phase).wait_recv()
            fill(1)

    def lat_rows(phase, k, c):
        part = pl.ds(c * 8, 8)
        n = phase * COMPS + k
        rows = [halo[n, 0, j, part] + corner_rows[k, 0, j, part] for j in range(3)]
        rows += [z_ref[k * ROWS + i, part] for i in range(ROWS)]
        rows += [halo[n, 1, j, part] + corner_rows[k, 1, j, part] for j in range(3)]
        out = []
        for i in range(ROWS):
            total = taps[0] * rows[i + 3]
            for j in range(1, 4):
                total = total + taps[j] * (rows[i + 3 - j] + rows[i + 3 + j])
            out.append(total)
        return out

    def ens_rows(plane, c, i):
        return ens[pl.ds(plane * TILE + c * 64 + i, 8, stride=ROWS), :]

    def reduce_first(n, value):
        part1[n, lat] = value

        @pl.loop(1, LAT)
        def _(o):
            ref = part1.at[n, lat]
            remote(ref, ref, red1_send.at[n], red1_recv.at[n], "lat", lat_peer(o)).start()

    def first_all(n):
        ref = part1.at[n, pl.ds(0, LAT - 1)]
        return remote(ref, ref, red1_send.at[n], red1_recv.at[n], "lat", lat_peer(1))

    def second_all(n):
        ref = part2.at[n, pl.ds(0, LON - 1)]
        return remote(ref, ref, red2_send.at[n], red2_recv.at[n], "lon", lon_peer(1))

    def reduce_second(n):
        first_all(n).wait_recv()
        total = part1[n, 0]
        for s in range(1, LAT):
            total = total + part1[n, s]
        part2[n, lon] = total

        @pl.loop(1, LON)
        def _(o):
            ref = part2.at[n, lon]
            remote(ref, ref, red2_send.at[n], red2_recv.at[n], "lon", lon_peer(o)).start()

    def reduce_last(n):
        second_all(n).wait_recv()
        total = part2[n, 0]
        for s in range(1, LON):
            total = total + part2[n, s]
        return total

    def rec1(o):
        return remote(rec_out1.at[lat_peer(o)], rec_in1.at[lat], rec1_send.at[0],
                      rec1_recv.at[0], "lat", lat_peer(o))

    def rec2(o):
        return remote(rec_out2.at[lon_peer(o)], rec_in2.at[lon], rec2_send.at[0],
                      rec2_recv.at[0], "lon", lon_peer(o))

    def rec1_all():
        return remote(rec_out1.at[pl.ds(0, LAT - 1)], rec_in1.at[pl.ds(0, LAT - 1)],
                      rec1_send.at[0], rec1_recv.at[0], "lat", lat_peer(1))

    def rec2_all():
        return remote(rec_out2.at[pl.ds(0, LON - 1)], rec_in2.at[pl.ds(0, LON - 1)],
                      rec2_send.at[0], rec2_recv.at[0], "lon", lon_peer(1))

    d_loads[0].wait()
    d_loads[1].wait()
    own_part(0, 0, d_rows)
    build_selections()
    pl.semaphore_wait(barrier, LAT + LON - 2)
    lat_start(0, 0)
    pack_records()

    @pl.loop(1, LAT)
    def _(o):
        rec1(o).start()

    rec_in1[lat] = rec_out1[lat]
    for copy in d_loads[2:]:
        copy.wait()
    own_part(0, 1, d_rows)
    lat_start(0, 1)
    pack_lon(0, d_rows)
    for copy in edge_copies(0):
        copy.start()
    for k in range(2, COMPS):
        own_part(0, k, d_rows)
        lat_start(0, k)

    rec1_all().wait_recv()

    @pl.loop(0, LON // 2)
    def _(p):
        rows = pl.ds(p * 2 * CAP, 2 * CAP)
        for s in range(LAT // 2):
            first, second = rec_in1[2 * s, rows], rec_in1[2 * s + 1, rows]
            rec_out2[2 * p, 8 * s:8 * s + 8] = jnp.concatenate([first[:CAP], second[:CAP]], 0)
            rec_out2[2 * p + 1, 8 * s:8 * s + 8] = jnp.concatenate([first[CAP:], second[CAP:]], 0)

    @pl.loop(1, LON)
    def _(o):
        rec2(o).start()

    rec_in2[lon] = rec_out2[lon]
    lon_part(0)
    ens_load.wait()

    @pl.loop(0, LEV)
    def _(n):
        ens[pl.ds(n * 64, 64), :] = ens16[pl.ds(n * 64, 64), :].astype(F32)

    ens[8 * TILE:9 * TILE, :] = 0.5 * std_ref[...].astype(F32)

    r_load.wait()

    def squares(n, carry):
        total_r, total_d = carry
        value_r = r_nat[pl.ds(n * 40, 40), :]
        value_d = d_nat[pl.ds(n * 40, 40), :]
        for s in range(5):
            piece = value_r[s * 8:s * 8 + 8]
            total_r = total_r + piece * piece
            piece = value_d[s * 8:s * 8 + 8]
            total_d = total_d + piece * piece
        return total_r, total_d

    sum_r, sum_d = lax.fori_loop(0, LEV, squares, (zeros8, zeros8))
    rec2_all().wait_recv()

    records = rec_in2[...].reshape(LAT * LON * CAP, CELLS)
    high, low = split(records.T)
    rec_t[...] = jnp.concatenate([high, low], 0)
    cell = records[:, LEV:].astype(jnp.int32)

    @pl.loop(0, ROWS)
    def _(p):
        hit = cell == iota((LAT * LON * CAP, 2 * CELLS), 1) + p * 2 * CELLS
        both = mxu(rec_t[...], jnp.where(hit, 1.0, 0.0).astype(BF16))
        total = both[:CELLS] + both[CELLS:]
        dens[2 * p] = total[:, :CELLS]
        dens[2 * p + 1] = total[:, CELLS:]

    @pl.loop(0, 2 * ROWS)
    def _(q):
        inc[q] = jnp.zeros((CELLS, CELLS), F32)

    corner_part(0)

    @pl.loop(0, MEMBERS)
    def _(k):
        lat_arrived(0, k)

        @pl.loop(0, CELLS // 8)
        def _(c):
            rows = lat_rows(0, k, c)
            for t in range(2):
                for i in range(ROWS):
                    inc[t * ROWS + i, pl.ds(c * 8, 8)] += ens_rows(2 * k + t, c, i) * rows[i]

    lat_arrived(0, MEMBERS)

    def adjoint(c, curve):
        rows = lat_rows(0, MEMBERS, c)
        part = pl.ds(c * 8, 8)
        for i in range(ROWS):
            spread = ens_rows(8, c, i)
            static = spread * rows[i]
            inc0 = inc[i, part] + static
            inc1 = inc[ROWS + i, part] + static
            back0 = dens[i, part] * inc0
            back1 = dens[ROWS + i, part] * inc1
            curve = curve + back0 * inc0 + back1 * inc1
            for m in range(MEMBERS):
                x_ref[m * ROWS + i, part] = (
                    ens_rows(2 * m, c, i) * back0 + ens_rows(2 * m + 1, c, i) * back1
                )
            x_ref[MEMBERS * ROWS + i, part] = spread * (back0 + back1)
        return curve

    curve = lax.fori_loop(0, CELLS // 8, adjoint, sum_d)
    lat_sent(0)
    for k in range(COMPS):
        own_part(1, k, x_rows)
        lat_start(1, k)
        if k == 0:
            pack_lon(1, x_rows)
            for copy in edge_copies(1):
                copy.start()
        if k == 1:
            sums = jnp.where(
                iota((8, CELLS), 0) == 0, jnp.sum(sum_r, axis=0, keepdims=True),
                jnp.where(
                    iota((8, CELLS), 0) == 1, jnp.sum(curve, axis=0, keepdims=True), 0.0
                ),
            )
            reduce_first(0, sums)
    reduce_second(0)
    lon_part(1)
    sums = reduce_last(0)
    norm_now = jnp.sum(sums[0:1], keepdims=True)
    alpha = norm_now / jnp.sum(sums[1:2], keepdims=True)

    c_load.wait()

    @pl.loop(0, LEV)
    def _(n):
        part = pl.ds(n * 40, 40)
        control_ref[part, :] = c_nat[part, :] + alpha * d_nat[part, :]

    corner_part(1)

    def update(k, total):
        lat_arrived(1, k)

        def body(c, total, height=8):
            rows = lat_rows(1, k, c)
            for i in range(ROWS):
                at = pl.ds(k * TILE + c * 64 + i, height, stride=ROWS)
                value = r_nat[at, :] - alpha * (d_nat[at, :] + rows[i][:height])
                residual_ref[at, :] = value
                total[height] = total[height] + value * value
            return total

        total = lax.fori_loop(0, LEV // 8, body, total)
        return body(LEV // 8, total, LEV % 8)

    def finish(n, carry):
        part = pl.ds(n * 40, 40)
        direction_ref[part, :] = residual_ref[part, :] + beta * d_nat[part, :]
        return carry

    total = lax.fori_loop(0, COMPS, update, {8: zeros8, 7: zeros8[:7]})
    last = jnp.concatenate([total[7], jnp.zeros((1, CELLS), F32)], 0)
    reduce_first(1, total[8] + last)
    reduce_second(1)
    norm_next = jnp.sum(reduce_last(1), keepdims=True)
    beta = norm_next / norm_now
    lax.fori_loop(0, LEV, finish, 0)

    lat_sent(1)
    for phase in range(2):
        for copy in edge_copies(phase):
            copy.wait_send()

        @pl.when(lat > 0)
        def _():
            corner_north(phase).wait_send()

        @pl.when(lat < LAT - 1)
        def _():
            corner_south(phase).wait_send()

        first_all(phase).wait_send()
        second_all(phase).wait_send()
    rec1_all().wait_send()
    rec2_all().wait_send()


def on_device(
    control, residual, direction, ensemble, static_std, vertical, owner, column, slot, corner,
    obs_weight, live_count,
):
    flat = (COMPS * TILE, CELLS)
    vmem = pl.BlockSpec(memory_space=pltpu.VMEM)
    hbm = pl.BlockSpec(memory_space=pltpu.HBM)
    dma = pltpu.SemaphoreType.DMA
    tail = (COMPS * TILE + ROWS, CELLS)
    square = (CELLS, CELLS)
    results = pl.pallas_call(
        kernel,
        out_shape=(pltpu.VMEM(flat, F32),) * 3,
        in_specs=[hbm] * 12,
        out_specs=(vmem,) * 3,
        scratch_shapes=[
            pltpu.VMEM((1, 1), jnp.int32),
            pltpu.VMEM((1, RECORDS), jnp.int32),
            pltpu.VMEM((1, RECORDS), jnp.int32),
            pltpu.VMEM((1, RECORDS), jnp.int32),
            pltpu.VMEM((4, RECORDS), jnp.int32),
            pltpu.VMEM((RECORDS, LEV), F32),
            pltpu.VMEM((TILE, CELLS), BF16),
            pltpu.VMEM((LEV, LEV), F32),
            pltpu.VMEM(tail, F32),
            pltpu.VMEM(tail, F32),
            pltpu.VMEM(flat, F32),
            pltpu.VMEM((8 * TILE, CELLS), BF16),
            pltpu.VMEM((9 * TILE + ROWS, CELLS), F32),
            pltpu.VMEM((COMPS * ROWS,) + square, F32),
            pltpu.VMEM((COMPS * ROWS,) + square, F32),
            pltpu.VMEM((COMPS * ROWS,) + square, F32),
            pltpu.VMEM((2 * COMPS, 2, 3) + square, F32),
            pltpu.VMEM((COMPS, 2, 3) + square, F32),
            pltpu.VMEM((2, 2) + square, F32),
            pltpu.VMEM((2, 2) + square, F32),
            pltpu.VMEM((2, 2) + square, F32),
            pltpu.VMEM((2, 2) + square, F32),
            pltpu.VMEM((2 * ROWS,) + square, F32),
            pltpu.VMEM((2 * ROWS,) + square, F32),
            pltpu.VMEM(square, F32),
            pltpu.VMEM((2, 2 * CELLS, 2 * CELLS), BF16),
            pltpu.VMEM((2 * CELLS, 2 * CELLS), BF16),
            pltpu.VMEM((2, 2 * CELLS, 2 * CELLS), BF16),
            pltpu.VMEM((PAIRS, 2 * CELLS, 2 * CELLS), BF16),
            pltpu.VMEM((PAIRS, 2 * CELLS, 2 * CELLS), BF16),
            pltpu.VMEM((8, 2 * CELLS, 2 * CELLS), BF16),
            pltpu.VMEM((LAT, LON * CAP, CELLS), F32),
            pltpu.VMEM((LAT, LON * CAP, CELLS), F32),
            pltpu.VMEM((LON, LAT * CAP, CELLS), F32),
            pltpu.VMEM((LON, LAT * CAP, CELLS), F32),
            pltpu.VMEM((2 * CELLS, LAT * LON * CAP), BF16),
            pltpu.VMEM((2, LAT, 8, CELLS), F32),
            pltpu.VMEM((2, LON, 8, CELLS), F32),
            dma((8,)),
            dma((COMPS,)),
            dma((3,)),
            dma((2, 2)), dma((2, 2)),
            dma((2, 2)), dma((2, 2)),
            dma((2 * COMPS, 2)), dma((2 * COMPS, 2)),
            dma((1,)), dma((1,)),
            dma((1,)), dma((1,)),
            dma((2,)), dma((2,)),
            dma((2,)), dma((2,)),
        ],
        compiler_params=pltpu.CompilerParams(
            collective_id=0, has_side_effects=True, vmem_limit_bytes=55 * 1024 * 1024
        ),
        name="analysis_step",
    )(
        live_count.reshape(1, 1),
        owner.reshape(1, RECORDS),
        column.reshape(1, RECORDS),
        slot.reshape(1, RECORDS),
        corner.T,
        obs_weight,
        static_std.reshape(TILE, CELLS),
        vertical,
        direction.reshape(flat),
        residual.reshape(flat),
        ensemble.reshape(8 * TILE, CELLS),
        control.reshape(flat),
    )
    return tuple(result.reshape(control.shape) for result in results)


def solution(mesh):
    field = P(None, None, "lat", "lon")
    return jax.shard_map(
        on_device,
        mesh=mesh,
        in_specs=(
            field,
            field,
            field,
            P(None, None, None, "lat", "lon"),
            P(None, "lat", "lon"),
            P(),
            P(("lon", "lat"), None),
            P(("lon", "lat")),
            P(("lon", "lat")),
            P(("lon", "lat"), None),
            P(("lon", "lat"), None),
            P(("lon", "lat")),
        ),
        out_specs=(field, field, field),
        check_vma=False,
    )
```

```python
import math

import jax
import jax.numpy as jnp
from jax import lax
from jax.experimental import pallas as pl
from jax.experimental.pallas import tpu as pltpu
from jax.sharding import PartitionSpec as P

LEV = 127
COMPS = 5
MEMBERS = 4
ROWS = 8
CELLS = 128
TILE = LEV * ROWS
LAT = 8
LON = 16
RECORDS = 256
CAP = 4
PAIRS = COMPS * ROWS // 2
PACKED = [(q % COMPS) * ROWS + q // COMPS for q in range(COMPS * ROWS)]
EDGE = 3 * 3 * COMPS
EARLY = 3
F32 = jnp.float32
BF16 = jnp.bfloat16


def filter_taps():
    raw = [math.exp(-(offset * offset) / 8.0) for offset in range(-3, 4)]
    scale = math.sqrt(sum(value * value for value in raw))
    return [value / scale for value in raw[3:]]


def iota(shape, dim):
    return lax.broadcasted_iota(jnp.int32, shape, dim)


def split(value):
    high = value.astype(BF16)
    return high, (value - high.astype(F32)).astype(BF16)


def mxu(a, b):
    return lax.dot_general(a, b, (((1,), (0,)), ((), ())), preferred_element_type=F32)


def level_matrix(matrix):
    high, low = split(matrix)
    return jnp.concatenate(
        [jnp.concatenate([high, high], 1), jnp.concatenate([low, jnp.zeros_like(low)], 1)], 0
    )


def lane_matrix(matrix):
    high, low = split(matrix)
    return jnp.concatenate(
        [jnp.concatenate([high, low], 1), jnp.concatenate([high, jnp.zeros_like(low)], 1)], 0
    )


def level_product(matrix, field):
    high, low = split(field)
    both = mxu(matrix, jnp.concatenate([high, low], 0))
    return both[:CELLS] + both[CELLS:]


def lane_product(field, matrix):
    high, low = split(field)
    both = mxu(jnp.concatenate([high, low], 1), matrix)
    return both[:, :CELLS] + both[:, CELLS:]


def kernel(
    live_hbm, owner_hbm, column_hbm, slot_hbm, corner_hbm, weight_hbm, std_hbm, v_hbm,
    d_hbm, r_hbm, ens_hbm, c_hbm,
    control_ref, residual_ref, direction_ref,
    live_ref, owner_ref, column_ref, slot_ref, corner_ref, weight_ref, std_ref, v_ref,
    d_nat, r_nat, c_nat, ens16, ens, x_ref, y_ref, z_ref, halo, corner_rows, lon_out, lon_in,
    corner_out, corner_in, inc, dens,
    vpad, level_w, lane_w, edge_w, pack_w, spread_w, corner_w, rec_out1, rec_in1, rec_out2, rec_in2, rec_t,
    part1, part2,
    small_sem, d_sem, load_sem, lon_send, lon_recv, corner_send, corner_recv, lat_send, lat_recv,
    rec1_send, rec1_recv, rec2_send, rec2_recv, red1_send, red1_recv, red2_send, red2_recv,
):
    lon = lax.axis_index("lon")
    lat = lax.axis_index("lat")
    taps = filter_taps()
    lane = iota((CELLS, CELLS), 1)

    def lat_peer(o):
        return lax.rem(lat + o, LAT)

    def lon_peer(o):
        return lax.rem(lon + o, LON)

    east, west = lon_peer(1), lon_peer(LON - 1)

    def remote(src, dst, send, recv, axis, peer):
        return pltpu.make_async_remote_copy(
            src_ref=src, dst_ref=dst, send_sem=send, recv_sem=recv,
            device_id={axis: peer}, device_id_type=pl.DeviceIdType.MESH,
        )

    barrier = pltpu.get_barrier_semaphore()

    @pl.loop(1, LAT)
    def _(o):
        pl.semaphore_signal(
            barrier, inc=1, device_id={"lat": lat_peer(o)}, device_id_type=pl.DeviceIdType.MESH
        )

    @pl.loop(1, LON)
    def _(o):
        pl.semaphore_signal(
            barrier, inc=1, device_id={"lon": lon_peer(o)}, device_id_type=pl.DeviceIdType.MESH
        )

    d_loads = [
        pltpu.make_async_copy(
            d_hbm.at[pl.ds(k * TILE, TILE)], d_nat.at[pl.ds(k * TILE, TILE)], d_sem.at[k]
        )
        for k in range(COMPS)
    ]
    ens_load = pltpu.make_async_copy(ens_hbm, ens16, load_sem.at[0])
    r_load = pltpu.make_async_copy(r_hbm, r_nat.at[pl.ds(0, COMPS * TILE)], load_sem.at[1])
    c_load = pltpu.make_async_copy(c_hbm, c_nat, load_sem.at[2])
    small_loads = [
        pltpu.make_async_copy(src, dst, small_sem.at[n])
        for n, (src, dst) in enumerate((
            (live_hbm, live_ref), (owner_hbm, owner_ref), (column_hbm, column_ref),
            (slot_hbm, slot_ref), (corner_hbm, corner_ref), (v_hbm, v_ref),
            (weight_hbm, weight_ref), (std_hbm, std_ref),
        ))
    ]
    small_loads[5].start()
    for copy in d_loads:
        copy.start()
    for n, copy in enumerate(small_loads):
        if n != 5:
            copy.start()
    ens_load.start()
    r_load.start()
    c_load.start()

    zeros8 = jnp.zeros((ROWS, CELLS), F32)
    d_nat[COMPS * TILE:, :] = zeros8
    r_nat[COMPS * TILE:, :] = zeros8
    ens[9 * TILE:, :] = zeros8
    vpad[...] = jnp.zeros((CELLS, CELLS), F32)

    small_loads[5].wait()
    vpad[0:LEV, 0:LEV] = v_ref[...]
    level_w[0] = level_matrix(vpad[...])
    level_w[1] = level_matrix(vpad[...].T)
    gap = jnp.abs(iota((CELLS, CELLS), 0) - lane)
    inner = jnp.zeros((CELLS, CELLS), F32)
    for k in range(4):
        inner = jnp.where(gap == k, taps[k], inner)
    lane_w[...] = lane_matrix(inner)

    def build_selections():
        part = iota((2 * CELLS, 2 * CELLS), 0) & (CELLS - 1)
        cells = iota((2 * CELLS, 2 * CELLS), 1)
        column = cells & (CELLS - 1)
        wanted = jnp.where(
            (column < 3) & (part < CELLS // 2), part - column,
            jnp.where(
                (column >= CELLS - 3) & (part >= CELLS // 2),
                part - CELLS // 2 - (column - (CELLS - 3)), -1000,
            ),
        ) - 3 * (cells >> 7)

        @pl.loop(0, 8)
        def _(p):
            corner_w[p] = jnp.where(wanted == 6 * p, 1.0, 0.0).astype(BF16)

        high_dim, low_dim = iota((2 * CELLS, 2 * CELLS), 0), iota((2 * CELLS, 2 * CELLS), 1)

        def selection(cell, packed, first, last):
            column, half = cell & (CELLS - 1), cell >> 7
            where = jnp.where(
                (column >= CELLS - 3) & (packed >= last) & (packed < last + CELLS),
                packed - last - (column - (CELLS - 3)),
                jnp.where(
                    (column < 3) & (packed >= first) & (packed < first + CELLS),
                    packed - first - column, -1000,
                ),
            )
            return where - 3 * half

        to_pack = selection(high_dim, low_dim, CELLS, 0)
        to_cell = selection(low_dim, high_dim, 0, CELLS)

        @pl.loop(0, PAIRS)
        def _(p):
            pack_w[p] = jnp.where(to_pack == 6 * p, 1.0, 0.0).astype(BF16)
            spread_w[p] = jnp.where(to_cell == 6 * p, 1.0, 0.0).astype(BF16)

        third = ((high_dim & (CELLS - 1)) * 43691) >> 17
        same = (third == ((low_dim & (CELLS - 1)) * 43691) >> 17) & (high_dim >> 7 == low_dim >> 7)
        step = jnp.where(high_dim < CELLS, high_dim - low_dim, low_dim - high_dim)
        edge = jnp.zeros((2 * CELLS, 2 * CELLS), F32)
        for k in range(1, 4):
            edge = jnp.where(same & (step == 3 - k), taps[k], edge)
        edge_w[0], edge_w[1] = split(edge)

    def pack_records():
        for n, copy in enumerate(small_loads):
            if n != 5:
                copy.wait()
        eye = iota((RECORDS, RECORDS), 0) == iota((RECORDS, RECORDS), 1)
        before = iota((RECORDS, RECORDS), 0) < iota((RECORDS, RECORDS), 1)
        owner = owner_ref[...]
        owner_col = jnp.sum(jnp.where(eye, owner, 0), axis=1, keepdims=True)
        rank = jnp.sum(jnp.where((owner_col == owner) & before, 1, 0), axis=0, keepdims=True)
        corner = corner_ref[...]
        place = (
            slot_ref[...] * (ROWS * CELLS) + column_ref[...]
            + corner[1:2] + CELLS * corner[2:3] + (CELLS + 1) * corner[3:4]
        )
        place_col = jnp.sum(jnp.where(eye, place, 0), axis=1, keepdims=True).astype(F32)
        target = (((owner & (LAT - 1)) * LON + (owner >> 3)) * CAP) + rank
        target = jnp.where(iota((1, RECORDS), 1) < live_ref[...], target, -1)
        chosen = jnp.where(iota((LAT * LON * CAP, RECORDS), 0) == target, 1.0, 0.0).astype(BF16)
        weights = jnp.concatenate([weight_ref[...], place_col], 1)
        high = weights.astype(BF16)
        mid = (weights - high.astype(F32)).astype(BF16)
        packed = mxu(chosen, jnp.concatenate([high, mid], 1))
        packed = packed[:, :CELLS] + packed[:, CELLS:]
        for s in range(LAT):
            rec_out1[s] = packed[s * LON * CAP:(s + 1) * LON * CAP]

    def blank(side):
        @pl.loop(0, 2 * COMPS)
        def _(n):
            halo[n, side] = jnp.zeros((3, CELLS, CELLS), F32)

        @pl.loop(0, COMPS)
        def _(k):
            corner_rows[k, side] = jnp.zeros((3, CELLS, CELLS), F32)

    @pl.when(lat == 0)
    def _():
        blank(0)

    @pl.when(lat == LAT - 1)
    def _():
        blank(1)

    def d_rows(q):
        k, i = q // ROWS, q % ROWS
        return d_nat[pl.ds(k * TILE + i, CELLS, stride=ROWS), :]

    def x_rows(q):
        return x_ref[q]

    def pack_lon(phase, rows):
        total = None
        for k in range(COMPS):
            value = jnp.concatenate([rows(PACKED[k * ROWS + i]) for i in range(ROWS)], 1)
            high, low = split(value)
            weight = pack_w[4 * k:4 * k + 4].reshape(ROWS * CELLS, 2 * CELLS)
            part = mxu(jnp.concatenate([high, low], 0), weight)
            total = part if total is None else total + part
        total = total[:CELLS] + total[CELLS:]
        lon_out[phase, 0] = total[:, :CELLS]
        lon_out[phase, 1] = total[:, CELLS:]

    def edge_copies(phase):
        return [
            remote(lon_out.at[phase, side], lon_in.at[phase, side], lon_send.at[phase, side],
                   lon_recv.at[phase, side], "lon", (east, west)[side])
            for side in range(2)
        ]

    def corner_north(phase):
        return remote(corner_out.at[phase, 0], corner_in.at[phase, 1], corner_send.at[phase, 1],
                      corner_recv.at[phase, 1], "lat", lax.rem(lat + LAT - 1, LAT))

    def corner_south(phase):
        return remote(corner_out.at[phase, 1], corner_in.at[phase, 0], corner_send.at[phase, 0],
                      corner_recv.at[phase, 0], "lat", lax.rem(lat + 1, LAT))

    def lat_north(phase, k):
        n = phase * COMPS + k
        return remote(y_ref.at[pl.ds(k * ROWS, 3)], halo.at[n, 1], lat_send.at[n, 1],
                      lat_recv.at[n, 1], "lat", lax.rem(lat + LAT - 1, LAT))

    def lat_south(phase, k):
        n = phase * COMPS + k
        return remote(y_ref.at[pl.ds(k * ROWS + 5, 3)], halo.at[n, 0], lat_send.at[n, 0],
                      lat_recv.at[n, 0], "lat", lax.rem(lat + 1, LAT))

    def lat_start(phase, k):
        @pl.when(lat > 0)
        def _():
            lat_north(phase, k).start()

        @pl.when(lat < LAT - 1)
        def _():
            lat_south(phase, k).start()

    def lat_arrived(phase, k):
        @pl.when(lat > 0)
        def _():
            lat_south(phase, k).wait_recv()

        @pl.when(lat < LAT - 1)
        def _():
            lat_north(phase, k).wait_recv()

    def lat_sent(phase):
        @pl.loop(0, COMPS)
        def _(k):
            @pl.when(lat > 0)
            def _():
                lat_north(phase, k).wait_send()

            @pl.when(lat < LAT - 1)
            def _():
                lat_south(phase, k).wait_send()

    def own_part(phase, k, rows):
        value = jnp.concatenate([rows(k * ROWS + i) for i in range(ROWS)], 1)
        value = level_product(level_w[phase], value)
        value = jnp.concatenate([value[:, i * CELLS:(i + 1) * CELLS] for i in range(ROWS)], 0)
        value = lane_product(value, lane_w[...])
        for i in range(ROWS):
            y_ref[k * ROWS + i] = value[i * CELLS:(i + 1) * CELLS]

    def lon_part(phase):
        for copy in edge_copies(phase):
            copy.wait_recv()
        edges = jnp.concatenate([lon_in[phase, 0], lon_in[phase, 1]], 1)
        high, low = split(level_product(level_w[phase], edges))
        both = mxu(jnp.concatenate([high, low], 0), edge_w[0])
        edges = both[:CELLS] + both[CELLS:] + mxu(high, edge_w[1])
        left, right = edges[:, :CELLS], edges[:, CELLS:]
        half = CELLS // 2
        corner_out[phase, 0] = jnp.where(lane < half, left, pltpu.roll(right, half, 1))
        start = COMPS * ROWS * 3 - EDGE
        corner_out[phase, 1] = jnp.where(
            lane < half, pltpu.roll(left, CELLS - start, 1),
            pltpu.roll(right, CELLS + half - start, 1),
        )

        @pl.when(lat > 0)
        def _():
            corner_north(phase).start()

        @pl.when(lat < LAT - 1)
        def _():
            corner_south(phase).start()

        for k in range(EARLY, COMPS):
            lat_start(phase, k)
        high, low = split(edges)
        edges = jnp.concatenate([high, low], 0)
        for p in range(PAIRS):
            both = mxu(edges, spread_w[p])
            both = both[:CELLS] + both[CELLS:]
            for n in range(2):
                q = PACKED[2 * p + n]
                z_ref[q] = y_ref[q] + both[:, n * CELLS:(n + 1) * CELLS]

    def corner_part(phase):
        def fill(side):
            high, low = split(corner_in[phase, side])
            edges = jnp.concatenate([high, low], 1)
            for p in range(8):
                both = mxu(edges, corner_w[p])
                for n in range(2):
                    q = 2 * p + n
                    if q < 3 * COMPS:
                        corner_rows[q % COMPS, side, q // COMPS] = (
                            both[:, n * CELLS:(n + 1) * CELLS]
                        )

        @pl.when(lat > 0)
        def _():
            corner_south(phase).wait_recv()
            fill(0)

        @pl.when(lat < LAT - 1)
        def _():
            corner_north(phase).wait_recv()
            fill(1)

    def lat_rows(phase, k, c):
        part = pl.ds(c * 8, 8)
        n = phase * COMPS + k
        rows = [halo[n, 0, j, part] + corner_rows[k, 0, j, part] for j in range(3)]
        rows += [z_ref[k * ROWS + i, part] for i in range(ROWS)]
        rows += [halo[n, 1, j, part] + corner_rows[k, 1, j, part] for j in range(3)]
        out = []
        for i in range(ROWS):
            total = taps[0] * rows[i + 3]
            for j in range(1, 4):
                total = total + taps[j] * (rows[i + 3 - j] + rows[i + 3 + j])
            out.append(total)
        return out

    def ens_rows(plane, c, i):
        return ens[pl.ds(plane * TILE + c * 64 + i, 8, stride=ROWS), :]

    def reduce_first(n, value):
        part1[n, lat] = value

        @pl.loop(1, LAT)
        def _(o):
            ref = part1.at[n, lat]
            remote(ref, ref, red1_send.at[n], red1_recv.at[n], "lat", lat_peer(o)).start()

    def first_all(n):
        ref = part1.at[n, pl.ds(0, LAT - 1)]
        return remote(ref, ref, red1_send.at[n], red1_recv.at[n], "lat", lat_peer(1))

    def second_all(n):
        ref = part2.at[n, pl.ds(0, LON - 1)]
        return remote(ref, ref, red2_send.at[n], red2_recv.at[n], "lon", lon_peer(1))

    def reduce_second(n):
        first_all(n).wait_recv()
        total = part1[n, 0]
        for s in range(1, LAT):
            total = total + part1[n, s]
        part2[n, lon] = total

        @pl.loop(1, LON)
        def _(o):
            ref = part2.at[n, lon]
            remote(ref, ref, red2_send.at[n], red2_recv.at[n], "lon", lon_peer(o)).start()

    def reduce_last(n):
        second_all(n).wait_recv()
        total = part2[n, 0]
        for s in range(1, LON):
            total = total + part2[n, s]
        return total

    def rec1(o):
        return remote(rec_out1.at[lat_peer(o)], rec_in1.at[lat], rec1_send.at[0],
                      rec1_recv.at[0], "lat", lat_peer(o))

    def rec2(o):
        return remote(rec_out2.at[lon_peer(o)], rec_in2.at[lon], rec2_send.at[0],
                      rec2_recv.at[0], "lon", lon_peer(o))

    def rec1_all():
        return remote(rec_out1.at[pl.ds(0, LAT - 1)], rec_in1.at[pl.ds(0, LAT - 1)],
                      rec1_send.at[0], rec1_recv.at[0], "lat", lat_peer(1))

    def rec2_all():
        return remote(rec_out2.at[pl.ds(0, LON - 1)], rec_in2.at[pl.ds(0, LON - 1)],
                      rec2_send.at[0], rec2_recv.at[0], "lon", lon_peer(1))

    def weigh():
        rec2_all().wait_recv()

        records = rec_in2[...].reshape(LAT * LON * CAP, CELLS)
        high, low = split(records.T)
        rec_t[...] = jnp.concatenate([high, low], 0)
        cell = records[:, LEV:].astype(jnp.int32)

        @pl.loop(0, ROWS, unroll=4)
        def _(p):
            hit = cell == iota((LAT * LON * CAP, 2 * CELLS), 1) + p * 2 * CELLS
            both = mxu(rec_t[...], jnp.where(hit, 1.0, 0.0).astype(BF16))
            total = both[:CELLS] + both[CELLS:]
            dens[2 * p] = total[:, :CELLS]
            dens[2 * p + 1] = total[:, CELLS:]

    d_loads[0].wait()
    d_loads[1].wait()
    own_part(0, 0, d_rows)
    pack_records()
    pl.semaphore_wait(barrier, LAT + LON - 2)

    @pl.loop(1, LAT)
    def _(o):
        rec1(o).start()

    lat_start(0, 0)
    rec_in1[lat] = rec_out1[lat]
    for copy in d_loads[2:]:
        copy.wait()
    own_part(0, 1, d_rows)
    lat_start(0, 1)
    build_selections()
    pack_lon(0, d_rows)
    for copy in edge_copies(0):
        copy.start()
    own_part(0, 2, d_rows)
    lat_start(0, 2)
    rec1_all().wait_recv()

    @pl.loop(0, LON // 2)
    def _(p):
        rows = pl.ds(p * 2 * CAP, 2 * CAP)
        for s in range(LAT // 2):
            first, second = rec_in1[2 * s, rows], rec_in1[2 * s + 1, rows]
            rec_out2[2 * p, 8 * s:8 * s + 8] = jnp.concatenate([first[:CAP], second[:CAP]], 0)
            rec_out2[2 * p + 1, 8 * s:8 * s + 8] = jnp.concatenate([first[CAP:], second[CAP:]], 0)

    @pl.loop(1, LON)
    def _(o):
        rec2(o).start()

    rec_in2[lon] = rec_out2[lon]
    for k in range(3, COMPS):
        own_part(0, k, d_rows)
    lon_part(0)
    ens_load.wait()

    @pl.loop(0, LEV)
    def _(n):
        ens[pl.ds(n * 64, 64), :] = ens16[pl.ds(n * 64, 64), :].astype(F32)

    ens[8 * TILE:9 * TILE, :] = 0.5 * std_ref[...].astype(F32)

    r_load.wait()

    def squares(n, carry):
        total_r, total_d = carry
        value_r = r_nat[pl.ds(n * 40, 40), :]
        value_d = d_nat[pl.ds(n * 40, 40), :]
        for s in range(5):
            piece = value_r[s * 8:s * 8 + 8]
            total_r = total_r + piece * piece
            piece = value_d[s * 8:s * 8 + 8]
            total_d = total_d + piece * piece
        return total_r, total_d

    sum_r, sum_d = lax.fori_loop(0, LEV, squares, (zeros8, zeros8))
    @pl.loop(0, 2 * ROWS)
    def _(q):
        inc[q] = jnp.zeros((CELLS, CELLS), F32)

    corner_part(0)

    def gather(k):
        lat_arrived(0, k)

        @pl.loop(0, CELLS // 8, unroll=2)
        def _(c):
            rows = lat_rows(0, k, c)
            for t in range(2):
                for i in range(ROWS):
                    inc[t * ROWS + i, pl.ds(c * 8, 8)] += ens_rows(2 * k + t, c, i) * rows[i]

    pl.loop(0, 2)(gather)
    weigh()
    pl.loop(2, MEMBERS)(gather)
    lat_arrived(0, MEMBERS)

    def adjoint(c, curve):
        rows = lat_rows(0, MEMBERS, c)
        part = pl.ds(c * 8, 8)
        for i in range(ROWS):
            spread = ens_rows(8, c, i)
            static = spread * rows[i]
            inc0 = inc[i, part] + static
            inc1 = inc[ROWS + i, part] + static
            back0 = dens[i, part] * inc0
            back1 = dens[ROWS + i, part] * inc1
            curve = curve + back0 * inc0 + back1 * inc1
            for m in range(MEMBERS):
                x_ref[m * ROWS + i, part] = (
                    ens_rows(2 * m, c, i) * back0 + ens_rows(2 * m + 1, c, i) * back1
                )
            x_ref[MEMBERS * ROWS + i, part] = spread * (back0 + back1)
        return curve

    curve = lax.fori_loop(0, CELLS // 8, adjoint, sum_d, unroll=2)
    lat_sent(0)
    for k in range(COMPS):
        own_part(1, k, x_rows)
        if k < EARLY:
            lat_start(1, k)
        if k == 0:
            pack_lon(1, x_rows)
            for copy in edge_copies(1):
                copy.start()
        if k == 1:
            sums = jnp.where(
                iota((8, CELLS), 0) == 0, jnp.sum(sum_r, axis=0, keepdims=True),
                jnp.where(
                    iota((8, CELLS), 0) == 1, jnp.sum(curve, axis=0, keepdims=True), 0.0
                ),
            )
            reduce_first(0, sums)
    lon_part(1)
    reduce_second(0)
    sums = reduce_last(0)
    norm_now = jnp.sum(sums[0:1], keepdims=True)
    alpha = norm_now / jnp.sum(sums[1:2], keepdims=True)

    c_load.wait()

    @pl.loop(0, LEV)
    def _(n):
        part = pl.ds(n * 40, 40)
        control_ref[part, :] = c_nat[part, :] + alpha * d_nat[part, :]

    corner_part(1)

    def update(k, total):
        lat_arrived(1, k)

        def body(c, total, height=8):
            rows = lat_rows(1, k, c)
            for i in range(ROWS):
                at = pl.ds(k * TILE + c * 64 + i, height, stride=ROWS)
                value = r_nat[at, :] - alpha * (d_nat[at, :] + rows[i][:height])
                residual_ref[at, :] = value
                total[height] = total[height] + value * value
            return total

        total = lax.fori_loop(0, LEV // 8, body, total, unroll=3)
        return body(LEV // 8, total, LEV % 8)

    def finish(n, carry):
        part = pl.ds(n * 40, 40)
        direction_ref[part, :] = residual_ref[part, :] + beta * d_nat[part, :]
        return carry

    total = lax.fori_loop(0, COMPS, update, {8: zeros8, 7: zeros8[:7]})
    last = jnp.concatenate([total[7], jnp.zeros((1, CELLS), F32)], 0)
    reduce_first(1, total[8] + last)
    reduce_second(1)
    norm_next = jnp.sum(reduce_last(1), keepdims=True)
    beta = norm_next / norm_now
    lax.fori_loop(0, LEV, finish, 0, unroll=4)

    lat_sent(1)
    for phase in range(2):
        for copy in edge_copies(phase):
            copy.wait_send()

        @pl.when(lat > 0)
        def _():
            corner_north(phase).wait_send()

        @pl.when(lat < LAT - 1)
        def _():
            corner_south(phase).wait_send()

        first_all(phase).wait_send()
        second_all(phase).wait_send()
    rec1_all().wait_send()
    rec2_all().wait_send()


def on_device(
    control, residual, direction, ensemble, static_std, vertical, owner, column, slot, corner,
    obs_weight, live_count,
):
    flat = (COMPS * TILE, CELLS)
    vmem = pl.BlockSpec(memory_space=pltpu.VMEM)
    hbm = pl.BlockSpec(memory_space=pltpu.HBM)
    dma = pltpu.SemaphoreType.DMA
    tail = (COMPS * TILE + ROWS, CELLS)
    square = (CELLS, CELLS)
    results = pl.pallas_call(
        kernel,
        out_shape=(pltpu.VMEM(flat, F32),) * 3,
        in_specs=[hbm] * 12,
        out_specs=(vmem,) * 3,
        scratch_shapes=[
            pltpu.VMEM((1, 1), jnp.int32),
            pltpu.VMEM((1, RECORDS), jnp.int32),
            pltpu.VMEM((1, RECORDS), jnp.int32),
            pltpu.VMEM((1, RECORDS), jnp.int32),
            pltpu.VMEM((4, RECORDS), jnp.int32),
            pltpu.VMEM((RECORDS, LEV), F32),
            pltpu.VMEM((TILE, CELLS), BF16),
            pltpu.VMEM((LEV, LEV), F32),
            pltpu.VMEM(tail, F32),
            pltpu.VMEM(tail, F32),
            pltpu.VMEM(flat, F32),
            pltpu.VMEM((8 * TILE, CELLS), BF16),
            pltpu.VMEM((9 * TILE + ROWS, CELLS), F32),
            pltpu.VMEM((COMPS * ROWS,) + square, F32),
            pltpu.VMEM((COMPS * ROWS,) + square, F32),
            pltpu.VMEM((COMPS * ROWS,) + square, F32),
            pltpu.VMEM((2 * COMPS, 2, 3) + square, F32),
            pltpu.VMEM((COMPS, 2, 3) + square, F32),
            pltpu.VMEM((2, 2) + square, F32),
            pltpu.VMEM((2, 2) + square, F32),
            pltpu.VMEM((2, 2) + square, F32),
            pltpu.VMEM((2, 2) + square, F32),
            pltpu.VMEM((2 * ROWS,) + square, F32),
            pltpu.VMEM((2 * ROWS,) + square, F32),
            pltpu.VMEM(square, F32),
            pltpu.VMEM((2, 2 * CELLS, 2 * CELLS), BF16),
            pltpu.VMEM((2 * CELLS, 2 * CELLS), BF16),
            pltpu.VMEM((2, 2 * CELLS, 2 * CELLS), BF16),
            pltpu.VMEM((PAIRS, 2 * CELLS, 2 * CELLS), BF16),
            pltpu.VMEM((PAIRS, 2 * CELLS, 2 * CELLS), BF16),
            pltpu.VMEM((8, 2 * CELLS, 2 * CELLS), BF16),
            pltpu.VMEM((LAT, LON * CAP, CELLS), F32),
            pltpu.VMEM((LAT, LON * CAP, CELLS), F32),
            pltpu.VMEM((LON, LAT * CAP, CELLS), F32),
            pltpu.VMEM((LON, LAT * CAP, CELLS), F32),
            pltpu.VMEM((2 * CELLS, LAT * LON * CAP), BF16),
            pltpu.VMEM((2, LAT, 8, CELLS), F32),
            pltpu.VMEM((2, LON, 8, CELLS), F32),
            dma((8,)),
            dma((COMPS,)),
            dma((3,)),
            dma((2, 2)), dma((2, 2)),
            dma((2, 2)), dma((2, 2)),
            dma((2 * COMPS, 2)), dma((2 * COMPS, 2)),
            dma((1,)), dma((1,)),
            dma((1,)), dma((1,)),
            dma((2,)), dma((2,)),
            dma((2,)), dma((2,)),
        ],
        compiler_params=pltpu.CompilerParams(
            collective_id=0, has_side_effects=True, vmem_limit_bytes=55 * 1024 * 1024
        ),
        name="analysis_step",
    )(
        live_count.reshape(1, 1),
        owner.reshape(1, RECORDS),
        column.reshape(1, RECORDS),
        slot.reshape(1, RECORDS),
        corner.T,
        obs_weight,
        static_std.reshape(TILE, CELLS),
        vertical,
        direction.reshape(flat),
        residual.reshape(flat),
        ensemble.reshape(8 * TILE, CELLS),
        control.reshape(flat),
    )
    return tuple(result.reshape(control.shape) for result in results)


def solution(mesh):
    field = P(None, None, "lat", "lon")
    return jax.shard_map(
        on_device,
        mesh=mesh,
        in_specs=(
            field,
            field,
            field,
            P(None, None, None, "lat", "lon"),
            P(None, "lat", "lon"),
            P(),
            P(("lon", "lat"), None),
            P(("lon", "lat")),
            P(("lon", "lat")),
            P(("lon", "lat"), None),
            P(("lon", "lat"), None),
            P(("lon", "lat")),
        ),
        out_specs=(field, field, field),
        check_vma=False,
    )
```

```python
import math

import jax
import jax.numpy as jnp
from jax import lax
from jax.experimental import pallas as pl
from jax.experimental.pallas import tpu as pltpu
from jax.sharding import PartitionSpec as P

LEV = 127
COMPS = 5
MEMBERS = 4
ROWS = 8
CELLS = 128
TILE = LEV * ROWS
LAT = 8
LON = 16
RECORDS = 256
CAP = 4
PAIRS = COMPS * ROWS // 2
PACKED = [(q % COMPS) * ROWS + q // COMPS for q in range(COMPS * ROWS)]
EDGE = 3 * 3 * COMPS
EARLY = 3
F32 = jnp.float32
BF16 = jnp.bfloat16


def filter_taps():
    raw = [math.exp(-(offset * offset) / 8.0) for offset in range(-3, 4)]
    scale = math.sqrt(sum(value * value for value in raw))
    return [value / scale for value in raw[3:]]


def iota(shape, dim):
    return lax.broadcasted_iota(jnp.int32, shape, dim)


def split(value):
    high = value.astype(BF16)
    return high, (value - high.astype(F32)).astype(BF16)


def mxu(a, b):
    return lax.dot_general(a, b, (((1,), (0,)), ((), ())), preferred_element_type=F32)


def level_matrix(matrix):
    high, low = split(matrix)
    return jnp.concatenate(
        [jnp.concatenate([high, high], 1), jnp.concatenate([low, jnp.zeros_like(low)], 1)], 0
    )


def lane_matrix(matrix):
    high, low = split(matrix)
    return jnp.concatenate(
        [jnp.concatenate([high, low], 1), jnp.concatenate([high, jnp.zeros_like(low)], 1)], 0
    )


def level_product(matrix, field):
    high, low = split(field)
    both = mxu(matrix, jnp.concatenate([high, low], 0))
    return both[:CELLS] + both[CELLS:]


def lane_product(field, matrix):
    high, low = split(field)
    both = mxu(jnp.concatenate([high, low], 1), matrix)
    return both[:, :CELLS] + both[:, CELLS:]


def kernel(
    live_hbm, owner_hbm, column_hbm, slot_hbm, corner_hbm, weight_hbm, std_hbm, v_hbm,
    d_hbm, r_hbm, ens_hbm, c_hbm,
    control_ref, residual_ref, direction_ref,
    live_ref, owner_ref, column_ref, slot_ref, corner_ref, weight_ref, std_ref, v_ref,
    d_nat, r_nat, c_nat, ens16, ens, x_ref, y_ref, z_ref, halo, corner_rows, lon_out, lon_in,
    corner_out, corner_in, inc, dens,
    vpad, level_w, lane_w, edge_w, pack_w, spread_w, corner_w, rec_out1, rec_in1, rec_out2, rec_in2, rec_t,
    part1, part2,
    small_sem, d_sem, load_sem, lon_send, lon_recv, corner_send, corner_recv, lat_send, lat_recv,
    rec1_send, rec1_recv, rec2_send, rec2_recv, red1_send, red1_recv, red2_send, red2_recv,
):
    lon = lax.axis_index("lon")
    lat = lax.axis_index("lat")
    taps = filter_taps()
    lane = iota((CELLS, CELLS), 1)

    def lat_peer(o):
        return lax.rem(lat + o, LAT)

    def lon_peer(o):
        return lax.rem(lon + o, LON)

    east, west = lon_peer(1), lon_peer(LON - 1)

    def remote(src, dst, send, recv, axis, peer):
        return pltpu.make_async_remote_copy(
            src_ref=src, dst_ref=dst, send_sem=send, recv_sem=recv,
            device_id={axis: peer}, device_id_type=pl.DeviceIdType.MESH,
        )

    barrier = pltpu.get_barrier_semaphore()

    @pl.loop(1, LAT)
    def _(o):
        pl.semaphore_signal(
            barrier, inc=1, device_id={"lat": lat_peer(o)}, device_id_type=pl.DeviceIdType.MESH
        )

    @pl.loop(1, LON)
    def _(o):
        pl.semaphore_signal(
            barrier, inc=1, device_id={"lon": lon_peer(o)}, device_id_type=pl.DeviceIdType.MESH
        )

    d_loads = [
        pltpu.make_async_copy(
            d_hbm.at[pl.ds(k * TILE, TILE)], d_nat.at[pl.ds(k * TILE, TILE)], d_sem.at[k]
        )
        for k in range(COMPS)
    ]
    ens_load = pltpu.make_async_copy(ens_hbm, ens16, load_sem.at[0])
    r_load = pltpu.make_async_copy(r_hbm, r_nat.at[pl.ds(0, COMPS * TILE)], load_sem.at[1])
    c_load = pltpu.make_async_copy(c_hbm, c_nat, load_sem.at[2])
    small_loads = [
        pltpu.make_async_copy(src, dst, small_sem.at[n])
        for n, (src, dst) in enumerate((
            (live_hbm, live_ref), (owner_hbm, owner_ref), (column_hbm, column_ref),
            (slot_hbm, slot_ref), (corner_hbm, corner_ref), (v_hbm, v_ref),
            (weight_hbm, weight_ref), (std_hbm, std_ref),
        ))
    ]
    small_loads[5].start()
    for copy in d_loads:
        copy.start()
    for n, copy in enumerate(small_loads):
        if n != 5:
            copy.start()
    ens_load.start()
    r_load.start()
    c_load.start()

    zeros8 = jnp.zeros((ROWS, CELLS), F32)
    d_nat[COMPS * TILE:, :] = zeros8
    r_nat[COMPS * TILE:, :] = zeros8
    ens[9 * TILE:, :] = zeros8
    vpad[...] = jnp.zeros((CELLS, CELLS), F32)

    small_loads[5].wait()
    vpad[0:LEV, 0:LEV] = v_ref[...]
    level_w[0] = level_matrix(vpad[...])
    level_w[1] = level_matrix(vpad[...].T)
    gap = jnp.abs(iota((CELLS, CELLS), 0) - lane)
    inner = jnp.zeros((CELLS, CELLS), F32)
    for k in range(4):
        inner = jnp.where(gap == k, taps[k], inner)
    lane_w[...] = lane_matrix(inner)

    def build_selections():
        part = iota((2 * CELLS, 2 * CELLS), 0) & (CELLS - 1)
        cells = iota((2 * CELLS, 2 * CELLS), 1)
        column = cells & (CELLS - 1)
        wanted = jnp.where(
            (column < 3) & (part < CELLS // 2), part - column,
            jnp.where(
                (column >= CELLS - 3) & (part >= CELLS // 2),
                part - CELLS // 2 - (column - (CELLS - 3)), -1000,
            ),
        ) - 3 * (cells >> 7)

        @pl.loop(0, 8)
        def _(p):
            corner_w[p] = jnp.where(wanted == 6 * p, 1.0, 0.0).astype(BF16)

        high_dim, low_dim = iota((2 * CELLS, 2 * CELLS), 0), iota((2 * CELLS, 2 * CELLS), 1)

        def selection(cell, packed, first, last):
            column, half = cell & (CELLS - 1), cell >> 7
            where = jnp.where(
                (column >= CELLS - 3) & (packed >= last) & (packed < last + CELLS),
                packed - last - (column - (CELLS - 3)),
                jnp.where(
                    (column < 3) & (packed >= first) & (packed < first + CELLS),
                    packed - first - column, -1000,
                ),
            )
            return where - 3 * half

        to_pack = selection(high_dim, low_dim, CELLS, 0)
        to_cell = selection(low_dim, high_dim, 0, CELLS)

        @pl.loop(0, PAIRS)
        def _(p):
            pack_w[p] = jnp.where(to_pack == 6 * p, 1.0, 0.0).astype(BF16)
            spread_w[p] = jnp.where(to_cell == 6 * p, 1.0, 0.0).astype(BF16)

        third = ((high_dim & (CELLS - 1)) * 43691) >> 17
        same = (third == ((low_dim & (CELLS - 1)) * 43691) >> 17) & (high_dim >> 7 == low_dim >> 7)
        step = jnp.where(high_dim < CELLS, high_dim - low_dim, low_dim - high_dim)
        edge = jnp.zeros((2 * CELLS, 2 * CELLS), F32)
        for k in range(1, 4):
            edge = jnp.where(same & (step == 3 - k), taps[k], edge)
        edge_w[0], edge_w[1] = split(edge)

    def pack_records():
        for n, copy in enumerate(small_loads):
            if n != 5:
                copy.wait()
        eye = iota((RECORDS, RECORDS), 0) == iota((RECORDS, RECORDS), 1)
        before = iota((RECORDS, RECORDS), 0) < iota((RECORDS, RECORDS), 1)
        owner = owner_ref[...]
        owner_col = jnp.sum(jnp.where(eye, owner, 0), axis=1, keepdims=True)
        rank = jnp.sum(jnp.where((owner_col == owner) & before, 1, 0), axis=0, keepdims=True)
        corner = corner_ref[...]
        place = (
            slot_ref[...] * (ROWS * CELLS) + column_ref[...]
            + corner[1:2] + CELLS * corner[2:3] + (CELLS + 1) * corner[3:4]
        )
        place_col = jnp.sum(jnp.where(eye, place, 0), axis=1, keepdims=True).astype(F32)
        target = (((owner & (LAT - 1)) * LON + (owner >> 3)) * CAP) + rank
        target = jnp.where(iota((1, RECORDS), 1) < live_ref[...], target, -1)
        chosen = jnp.where(iota((LAT * LON * CAP, RECORDS), 0) == target, 1.0, 0.0).astype(BF16)
        weights = jnp.concatenate([weight_ref[...], place_col], 1)
        high = weights.astype(BF16)
        mid = (weights - high.astype(F32)).astype(BF16)
        packed = mxu(chosen, jnp.concatenate([high, mid], 1))
        packed = packed[:, :CELLS] + packed[:, CELLS:]
        for s in range(LAT):
            rec_out1[s] = packed[s * LON * CAP:(s + 1) * LON * CAP]

    def blank(side):
        @pl.loop(0, 2 * COMPS)
        def _(n):
            halo[n, side] = jnp.zeros((3, CELLS, CELLS), F32)

        @pl.loop(0, COMPS)
        def _(k):
            corner_rows[k, side] = jnp.zeros((3, CELLS, CELLS), F32)

    @pl.when(lat == 0)
    def _():
        blank(0)

    @pl.when(lat == LAT - 1)
    def _():
        blank(1)

    def d_rows(q):
        k, i = q // ROWS, q % ROWS
        return d_nat[pl.ds(k * TILE + i, CELLS, stride=ROWS), :]

    def x_rows(q):
        return x_ref[q]

    def pack_lon(phase, rows):
        total = None
        for k in range(COMPS):
            value = jnp.concatenate([rows(PACKED[k * ROWS + i]) for i in range(ROWS)], 1)
            high, low = split(value)
            weight = pack_w[4 * k:4 * k + 4].reshape(ROWS * CELLS, 2 * CELLS)
            part = mxu(jnp.concatenate([high, low], 0), weight)
            total = part if total is None else total + part
        total = total[:CELLS] + total[CELLS:]
        lon_out[phase, 0] = total[:, :CELLS]
        lon_out[phase, 1] = total[:, CELLS:]

    def edge_copies(phase):
        return [
            remote(lon_out.at[phase, side], lon_in.at[phase, side], lon_send.at[phase, side],
                   lon_recv.at[phase, side], "lon", (east, west)[side])
            for side in range(2)
        ]

    def corner_north(phase):
        return remote(corner_out.at[phase, 0], corner_in.at[phase, 1], corner_send.at[phase, 1],
                      corner_recv.at[phase, 1], "lat", lax.rem(lat + LAT - 1, LAT))

    def corner_south(phase):
        return remote(corner_out.at[phase, 1], corner_in.at[phase, 0], corner_send.at[phase, 0],
                      corner_recv.at[phase, 0], "lat", lax.rem(lat + 1, LAT))

    def lat_north(phase, k):
        n = phase * COMPS + k
        return remote(y_ref.at[pl.ds(k * ROWS, 3)], halo.at[n, 1], lat_send.at[n, 1],
                      lat_recv.at[n, 1], "lat", lax.rem(lat + LAT - 1, LAT))

    def lat_south(phase, k):
        n = phase * COMPS + k
        return remote(y_ref.at[pl.ds(k * ROWS + 5, 3)], halo.at[n, 0], lat_send.at[n, 0],
                      lat_recv.at[n, 0], "lat", lax.rem(lat + 1, LAT))

    def lat_start(phase, k):
        @pl.when(lat > 0)
        def _():
            lat_north(phase, k).start()

        @pl.when(lat < LAT - 1)
        def _():
            lat_south(phase, k).start()

    def lat_arrived(phase, k):
        @pl.when(lat > 0)
        def _():
            lat_south(phase, k).wait_recv()

        @pl.when(lat < LAT - 1)
        def _():
            lat_north(phase, k).wait_recv()

    def lat_sent(phase):
        @pl.loop(0, COMPS)
        def _(k):
            @pl.when(lat > 0)
            def _():
                lat_north(phase, k).wait_send()

            @pl.when(lat < LAT - 1)
            def _():
                lat_south(phase, k).wait_send()

    def own_part(phase, k, rows):
        value = jnp.concatenate([rows(k * ROWS + i) for i in range(ROWS)], 1)
        value = level_product(level_w[phase], value)
        value = jnp.concatenate([value[:, i * CELLS:(i + 1) * CELLS] for i in range(ROWS)], 0)
        value = lane_product(value, lane_w[...])
        for i in range(ROWS):
            y_ref[k * ROWS + i] = value[i * CELLS:(i + 1) * CELLS]

    def lon_part(phase):
        for copy in edge_copies(phase):
            copy.wait_recv()
        edges = jnp.concatenate([lon_in[phase, 0], lon_in[phase, 1]], 1)
        high, low = split(level_product(level_w[phase], edges))
        both = mxu(jnp.concatenate([high, low], 0), edge_w[0])
        edges = both[:CELLS] + both[CELLS:] + mxu(high, edge_w[1])
        left, right = edges[:, :CELLS], edges[:, CELLS:]
        half = CELLS // 2
        corner_out[phase, 0] = jnp.where(lane < half, left, pltpu.roll(right, half, 1))
        start = COMPS * ROWS * 3 - EDGE
        corner_out[phase, 1] = jnp.where(
            lane < half, pltpu.roll(left, CELLS - start, 1),
            pltpu.roll(right, CELLS + half - start, 1),
        )

        @pl.when(lat > 0)
        def _():
            corner_north(phase).start()

        @pl.when(lat < LAT - 1)
        def _():
            corner_south(phase).start()

        for k in range(EARLY, COMPS):
            lat_start(phase, k)
        high, low = split(edges)
        edges = jnp.concatenate([high, low], 0)
        for p in range(PAIRS):
            both = mxu(edges, spread_w[p])
            both = both[:CELLS] + both[CELLS:]
            for n in range(2):
                q = PACKED[2 * p + n]
                z_ref[q] = y_ref[q] + both[:, n * CELLS:(n + 1) * CELLS]

    def corner_part(phase):
        def fill(side):
            high, low = split(corner_in[phase, side])
            edges = jnp.concatenate([high, low], 1)
            for p in range(8):
                both = mxu(edges, corner_w[p])
                for n in range(2):
                    q = 2 * p + n
                    if q < 3 * COMPS:
                        corner_rows[q % COMPS, side, q // COMPS] = (
                            both[:, n * CELLS:(n + 1) * CELLS]
                        )

        @pl.when(lat > 0)
        def _():
            corner_south(phase).wait_recv()
            fill(0)

        @pl.when(lat < LAT - 1)
        def _():
            corner_north(phase).wait_recv()
            fill(1)

    def lat_rows(phase, k, c):
        part = pl.ds(c * 8, 8)
        n = phase * COMPS + k
        rows = [halo[n, 0, j, part] + corner_rows[k, 0, j, part] for j in range(3)]
        rows += [z_ref[k * ROWS + i, part] for i in range(ROWS)]
        rows += [halo[n, 1, j, part] + corner_rows[k, 1, j, part] for j in range(3)]
        out = []
        for i in range(ROWS):
            total = taps[0] * rows[i + 3]
            for j in range(1, 4):
                total = total + taps[j] * (rows[i + 3 - j] + rows[i + 3 + j])
            out.append(total)
        return out

    def ens_rows(plane, c, i):
        return ens[pl.ds(plane * TILE + c * 64 + i, 8, stride=ROWS), :]

    def reduce_first(n, value):
        part1[n, lat] = value

        @pl.loop(1, LAT)
        def _(o):
            ref = part1.at[n, lat]
            remote(ref, ref, red1_send.at[n], red1_recv.at[n], "lat", lat_peer(o)).start()

    def first_all(n):
        ref = part1.at[n, pl.ds(0, LAT - 1)]
        return remote(ref, ref, red1_send.at[n], red1_recv.at[n], "lat", lat_peer(1))

    def second_all(n):
        ref = part2.at[n, pl.ds(0, LON - 1)]
        return remote(ref, ref, red2_send.at[n], red2_recv.at[n], "lon", lon_peer(1))

    def reduce_second(n):
        first_all(n).wait_recv()
        total = part1[n, 0]
        for s in range(1, LAT):
            total = total + part1[n, s]
        part2[n, lon] = total

        @pl.loop(1, LON)
        def _(o):
            ref = part2.at[n, lon]
            remote(ref, ref, red2_send.at[n], red2_recv.at[n], "lon", lon_peer(o)).start()

    def reduce_last(n):
        second_all(n).wait_recv()
        total = part2[n, 0]
        for s in range(1, LON):
            total = total + part2[n, s]
        return total

    def rec1(o):
        return remote(rec_out1.at[lat_peer(o)], rec_in1.at[lat], rec1_send.at[0],
                      rec1_recv.at[0], "lat", lat_peer(o))

    def rec2(o):
        return remote(rec_out2.at[lon_peer(o)], rec_in2.at[lon], rec2_send.at[0],
                      rec2_recv.at[0], "lon", lon_peer(o))

    def rec1_all():
        return remote(rec_out1.at[pl.ds(0, LAT - 1)], rec_in1.at[pl.ds(0, LAT - 1)],
                      rec1_send.at[0], rec1_recv.at[0], "lat", lat_peer(1))

    def rec2_all():
        return remote(rec_out2.at[pl.ds(0, LON - 1)], rec_in2.at[pl.ds(0, LON - 1)],
                      rec2_send.at[0], rec2_recv.at[0], "lon", lon_peer(1))

    def weigh():
        rec2_all().wait_recv()

        records = rec_in2[...].reshape(LAT * LON * CAP, CELLS)
        high, low = split(records.T)
        rec_t[...] = jnp.concatenate([high, low], 0)
        cell = records[:, LEV:].astype(jnp.int32)

        @pl.loop(0, ROWS, unroll=4)
        def _(p):
            hit = cell == iota((LAT * LON * CAP, 2 * CELLS), 1) + p * 2 * CELLS
            both = mxu(rec_t[...], jnp.where(hit, 1.0, 0.0).astype(BF16))
            total = both[:CELLS] + both[CELLS:]
            dens[2 * p] = total[:, :CELLS]
            dens[2 * p + 1] = total[:, CELLS:]

    d_loads[0].wait()
    d_loads[1].wait()
    own_part(0, 0, d_rows)
    pack_records()
    pl.semaphore_wait(barrier, LAT + LON - 2)

    @pl.loop(1, LAT)
    def _(o):
        rec1(o).start()

    lat_start(0, 0)
    rec_in1[lat] = rec_out1[lat]
    for copy in d_loads[2:]:
        copy.wait()
    own_part(0, 1, d_rows)
    lat_start(0, 1)
    build_selections()
    pack_lon(0, d_rows)
    for copy in edge_copies(0):
        copy.start()
    own_part(0, 2, d_rows)
    lat_start(0, 2)
    rec1_all().wait_recv()

    @pl.loop(0, LON // 2)
    def _(p):
        rows = pl.ds(p * 2 * CAP, 2 * CAP)
        for s in range(LAT // 2):
            first, second = rec_in1[2 * s, rows], rec_in1[2 * s + 1, rows]
            rec_out2[2 * p, 8 * s:8 * s + 8] = jnp.concatenate([first[:CAP], second[:CAP]], 0)
            rec_out2[2 * p + 1, 8 * s:8 * s + 8] = jnp.concatenate([first[CAP:], second[CAP:]], 0)

    @pl.loop(1, LON)
    def _(o):
        rec2(o).start()

    rec_in2[lon] = rec_out2[lon]
    for k in range(3, COMPS):
        own_part(0, k, d_rows)
    lon_part(0)
    ens_load.wait()

    @pl.loop(0, LEV)
    def _(n):
        ens[pl.ds(n * 64, 64), :] = ens16[pl.ds(n * 64, 64), :].astype(F32)

    ens[8 * TILE:9 * TILE, :] = 0.5 * std_ref[...].astype(F32)

    r_load.wait()

    def squares(n, carry):
        total_r, total_d = carry
        value_r = r_nat[pl.ds(n * 40, 40), :]
        value_d = d_nat[pl.ds(n * 40, 40), :]
        for s in range(5):
            piece = value_r[s * 8:s * 8 + 8]
            total_r = total_r + piece * piece
            piece = value_d[s * 8:s * 8 + 8]
            total_d = total_d + piece * piece
        return total_r, total_d

    sum_r, sum_d = lax.fori_loop(0, LEV, squares, (zeros8, zeros8))
    @pl.loop(0, 2 * ROWS)
    def _(q):
        inc[q] = jnp.zeros((CELLS, CELLS), F32)

    corner_part(0)

    def gather(k):
        lat_arrived(0, k)

        @pl.loop(0, CELLS // 8, unroll=2)
        def _(c):
            rows = lat_rows(0, k, c)
            for t in range(2):
                for i in range(ROWS):
                    inc[t * ROWS + i, pl.ds(c * 8, 8)] += ens_rows(2 * k + t, c, i) * rows[i]

    pl.loop(0, 2)(gather)
    weigh()
    pl.loop(2, MEMBERS)(gather)
    lat_arrived(0, MEMBERS)

    def adjoint(c, curve):
        rows = lat_rows(0, MEMBERS, c)
        part = pl.ds(c * 8, 8)
        for i in range(ROWS):
            spread = ens_rows(8, c, i)
            static = spread * rows[i]
            inc0 = inc[i, part] + static
            inc1 = inc[ROWS + i, part] + static
            back0 = dens[i, part] * inc0
            back1 = dens[ROWS + i, part] * inc1
            curve = curve + back0 * inc0 + back1 * inc1
            for m in range(MEMBERS):
                x_ref[m * ROWS + i, part] = (
                    ens_rows(2 * m, c, i) * back0 + ens_rows(2 * m + 1, c, i) * back1
                )
            x_ref[MEMBERS * ROWS + i, part] = spread * (back0 + back1)
        return curve

    curve = lax.fori_loop(0, CELLS // 8, adjoint, sum_d, unroll=2)
    lat_sent(0)
    for k in range(COMPS):
        own_part(1, k, x_rows)
        if k < EARLY:
            lat_start(1, k)
        if k == 0:
            pack_lon(1, x_rows)
            for copy in edge_copies(1):
                copy.start()
        if k == 1:
            sums = jnp.where(
                iota((8, CELLS), 0) == 0, jnp.sum(sum_r, axis=0, keepdims=True),
                jnp.where(
                    iota((8, CELLS), 0) == 1, jnp.sum(curve, axis=0, keepdims=True), 0.0
                ),
            )
            reduce_first(0, sums)
    lon_part(1)
    reduce_second(0)
    sums = reduce_last(0)
    norm_now = jnp.sum(sums[0:1], keepdims=True)
    alpha = norm_now / jnp.sum(sums[1:2], keepdims=True)

    corner_part(1)

    def update(k, total):
        lat_arrived(1, k)

        def body(c, total, height=8):
            rows = lat_rows(1, k, c)
            for i in range(ROWS):
                at = pl.ds(k * TILE + c * 64 + i, height, stride=ROWS)
                value = r_nat[at, :] - alpha * (d_nat[at, :] + rows[i][:height])
                residual_ref[at, :] = value
                total[height] = total[height] + value * value
            return total

        total = lax.fori_loop(0, LEV // 8, body, total, unroll=3)
        return body(LEV // 8, total, LEV % 8)

    def finish(n, carry):
        part = pl.ds(n * 40, 40)
        direction_ref[part, :] = residual_ref[part, :] + beta * d_nat[part, :]
        return carry

    total = lax.fori_loop(0, COMPS, update, {8: zeros8, 7: zeros8[:7]})
    last = jnp.concatenate([total[7], jnp.zeros((1, CELLS), F32)], 0)
    reduce_first(1, total[8] + last)

    c_load.wait()

    @pl.loop(0, LEV)
    def _(n):
        part = pl.ds(n * 40, 40)
        control_ref[part, :] = c_nat[part, :] + alpha * d_nat[part, :]

    reduce_second(1)
    lat_sent(1)
    for phase in range(2):
        for copy in edge_copies(phase):
            copy.wait_send()

        @pl.when(lat > 0)
        def _():
            corner_north(phase).wait_send()

        @pl.when(lat < LAT - 1)
        def _():
            corner_south(phase).wait_send()

    first_all(0).wait_send()
    second_all(0).wait_send()
    rec1_all().wait_send()
    rec2_all().wait_send()

    norm_next = jnp.sum(reduce_last(1), keepdims=True)
    beta = norm_next / norm_now
    lax.fori_loop(0, LEV, finish, 0, unroll=4)
    first_all(1).wait_send()
    second_all(1).wait_send()


def on_device(
    control, residual, direction, ensemble, static_std, vertical, owner, column, slot, corner,
    obs_weight, live_count,
):
    flat = (COMPS * TILE, CELLS)
    vmem = pl.BlockSpec(memory_space=pltpu.VMEM)
    hbm = pl.BlockSpec(memory_space=pltpu.HBM)
    dma = pltpu.SemaphoreType.DMA
    tail = (COMPS * TILE + ROWS, CELLS)
    square = (CELLS, CELLS)
    results = pl.pallas_call(
        kernel,
        out_shape=(pltpu.VMEM(flat, F32),) * 3,
        in_specs=[hbm] * 12,
        out_specs=(vmem,) * 3,
        scratch_shapes=[
            pltpu.VMEM((1, 1), jnp.int32),
            pltpu.VMEM((1, RECORDS), jnp.int32),
            pltpu.VMEM((1, RECORDS), jnp.int32),
            pltpu.VMEM((1, RECORDS), jnp.int32),
            pltpu.VMEM((4, RECORDS), jnp.int32),
            pltpu.VMEM((RECORDS, LEV), F32),
            pltpu.VMEM((TILE, CELLS), BF16),
            pltpu.VMEM((LEV, LEV), F32),
            pltpu.VMEM(tail, F32),
            pltpu.VMEM(tail, F32),
            pltpu.VMEM(flat, F32),
            pltpu.VMEM((8 * TILE, CELLS), BF16),
            pltpu.VMEM((9 * TILE + ROWS, CELLS), F32),
            pltpu.VMEM((COMPS * ROWS,) + square, F32),
            pltpu.VMEM((COMPS * ROWS,) + square, F32),
            pltpu.VMEM((COMPS * ROWS,) + square, F32),
            pltpu.VMEM((2 * COMPS, 2, 3) + square, F32),
            pltpu.VMEM((COMPS, 2, 3) + square, F32),
            pltpu.VMEM((2, 2) + square, F32),
            pltpu.VMEM((2, 2) + square, F32),
            pltpu.VMEM((2, 2) + square, F32),
            pltpu.VMEM((2, 2) + square, F32),
            pltpu.VMEM((2 * ROWS,) + square, F32),
            pltpu.VMEM((2 * ROWS,) + square, F32),
            pltpu.VMEM(square, F32),
            pltpu.VMEM((2, 2 * CELLS, 2 * CELLS), BF16),
            pltpu.VMEM((2 * CELLS, 2 * CELLS), BF16),
            pltpu.VMEM((2, 2 * CELLS, 2 * CELLS), BF16),
            pltpu.VMEM((PAIRS, 2 * CELLS, 2 * CELLS), BF16),
            pltpu.VMEM((PAIRS, 2 * CELLS, 2 * CELLS), BF16),
            pltpu.VMEM((8, 2 * CELLS, 2 * CELLS), BF16),
            pltpu.VMEM((LAT, LON * CAP, CELLS), F32),
            pltpu.VMEM((LAT, LON * CAP, CELLS), F32),
            pltpu.VMEM((LON, LAT * CAP, CELLS), F32),
            pltpu.VMEM((LON, LAT * CAP, CELLS), F32),
            pltpu.VMEM((2 * CELLS, LAT * LON * CAP), BF16),
            pltpu.VMEM((2, LAT, 8, CELLS), F32),
            pltpu.VMEM((2, LON, 8, CELLS), F32),
            dma((8,)),
            dma((COMPS,)),
            dma((3,)),
            dma((2, 2)), dma((2, 2)),
            dma((2, 2)), dma((2, 2)),
            dma((2 * COMPS, 2)), dma((2 * COMPS, 2)),
            dma((1,)), dma((1,)),
            dma((1,)), dma((1,)),
            dma((2,)), dma((2,)),
            dma((2,)), dma((2,)),
        ],
        compiler_params=pltpu.CompilerParams(
            collective_id=0, has_side_effects=True, vmem_limit_bytes=55 * 1024 * 1024
        ),
        name="analysis_step",
    )(
        live_count.reshape(1, 1),
        owner.reshape(1, RECORDS),
        column.reshape(1, RECORDS),
        slot.reshape(1, RECORDS),
        corner.T,
        obs_weight,
        static_std.reshape(TILE, CELLS),
        vertical,
        direction.reshape(flat),
        residual.reshape(flat),
        ensemble.reshape(8 * TILE, CELLS),
        control.reshape(flat),
    )
    return tuple(result.reshape(control.shape) for result in results)


def solution(mesh):
    field = P(None, None, "lat", "lon")
    return jax.shard_map(
        on_device,
        mesh=mesh,
        in_specs=(
            field,
            field,
            field,
            P(None, None, None, "lat", "lon"),
            P(None, "lat", "lon"),
            P(),
            P(("lon", "lat"), None),
            P(("lon", "lat")),
            P(("lon", "lat")),
            P(("lon", "lat"), None),
            P(("lon", "lat"), None),
            P(("lon", "lat")),
        ),
        out_specs=(field, field, field),
        check_vma=False,
    )
```
